128 devices in a mesh: blk: 16 (over y, z), beam: 8 (over x, core).
Axes of the slice: x: 4, y: 4, z: 4, core: 2. Of those that a mesh axis runs over, the one named last changes fastest.
Arguments:
- signal: float32 [2097152], P(('blk', 'beam')), may hold values from -6 to 6
- weight: float32 [2097152], P(('blk', 'beam')), may hold values from 0.25 to 1
- cycle: int32 [2097152], P(('blk', 'beam')), may hold values from 0 to 1
- phi: int32 [2097152], P(('blk', 'beam')), may hold values from 0 to 2047
- psi: int32 [2097152], P(('blk', 'beam')), may hold values from 0 to 31
- owner: int32 [16384, 1], P(('blk', 'beam')), may hold values from 0 to 15; in each aligned block of 128 rows (0 to 127, 128 to 255, ...) at most 20 rows name the same one
- wigner: bfloat16 [1024, 32, 32, 1152], P('blk', 'beam'), may hold values from -0.25 to 0.25
Outputs:
- alm: float32 [1024, 2, 1152], P(('blk', 'beam'))
The draws below stay inside these ranges and needn't reach their ends.
Inputs may be any that keep to these rules, and one draw needn't show every extreme that they name: `owner`: among the 128 blocks of one device no cycle group is named by more than 20 blocks, and in some device's blocks one group is named by exactly 20.
All inputs are finite; a program needn't handle non-finite values.
Results may differ from the reference program's by a relative error of at most 0.02.
Values may be sent and summed in bfloat16 or wider, within the bound.
A program may use at most 128 MiB of HBM per device.

```python
import math
import jax
import jax.numpy as jnp
import numpy as np
from jax import lax

BLK_DEV = 128
BLOCK_ROWS = 128
CYCLE_DEV = 2
NPSI = 32
NPHI = 2048
L = 1152
CAP = 20
CYCLES = 32
NM = 1024
BLOCKS = 16384
SAMPLES = 2097152
N_BLK = 16


def with_ends(values, stream_key, least, top_value):
    spot = [jax.random.randint(jax.random.fold_in(stream_key, axis), (), 0, length) for axis, length in enumerate(values.shape)]
    longest = values.shape.index(max(values.shape))
    beside = spot[:longest] + [(spot[longest] + 1) % values.shape[longest]] + spot[longest + 1:]
    return values.at[tuple(spot)].set(least).at[tuple(beside)].set(top_value)


def strengthened(array, key, source, target, shards_of, factor):
    owner, partner = [(jnp.arange(array.shape[position]) // (array.shape[position] // shards_of)).reshape([-1 if axis == position else 1 for axis in range(array.ndim)]) for position in (source, target)]
    chosen = jax.random.permutation(key, shards_of)[partner]
    strong = (owner == chosen) | (owner == (partner + shards_of // 2) % shards_of)
    return jnp.where(strong, factor * array, array)


def level_of(key, dims, shards, low, largest):
    loudness, own = 1.0, jax.random.fold_in(key, 6)
    for dim, parts in shards:
        draws = jnp.exp(jax.random.uniform(jax.random.fold_in(own, dim), (parts,), jnp.float32, low / len(shards), largest / len(shards)))
        loudness = loudness * jnp.repeat(draws, dims[dim] // parts).reshape([-1 if axis == dim else 1 for axis in range(len(dims))])
    return loudness


def deal_out(own_key, own, number, rows, count, top, limit, skew):
    ranking = jax.random.permutation(own_key, count)
    crowded, usual = shares(count, rows * top, limit, skew, True), shares(count, rows * top, limit, skew, False)
    places = jnp.arange(count)

    def named(tallies, rotation):
        used = int((tallies > 0).sum())
        fixed = max(1, used // 4)
        shifted = fixed + (places - fixed + rotation * (used - fixed)) % max(1, count - fixed)
        return jnp.zeros((count,), jnp.int32).at[ranking[jnp.where(places < fixed, places, shifted)]].set(jnp.asarray(tallies, jnp.int32))

    tallies = jnp.where(number % 4 == 0, named(crowded, number // 4), named(usual, number - number // 4 - 1))
    mixed = jax.random.permutation(jax.random.fold_in(own, 3), count)
    donor, sink = mixed[0:count // 2 * 2:2], mixed[1:count // 2 * 2:2]
    margin = jnp.minimum(tallies[donor] - 1, limit - tallies[sink]) // 2
    margin = jnp.where((donor == ranking[0]) | (sink == ranking[0]) | (tallies[sink] == 0), 0, jnp.maximum(margin, 0))
    shifted = jax.random.randint(jax.random.fold_in(own, 4), (count // 2,), 0, 1 << 20) % (margin + 1)
    tallies = tallies.at[donor].add(-shifted).at[sink].add(shifted)
    items = jnp.searchsorted(jnp.cumsum(tallies), jnp.arange(rows * top), side="right").astype(jnp.int32)
    table = items.reshape(top, rows).T
    table = table[jax.random.permutation(jax.random.fold_in(own, 1), rows)]
    rotation = jax.random.randint(jax.random.fold_in(own, 2), (rows, 1), 0, top)
    return jnp.take_along_axis(table, (jnp.arange(top)[None, :] + rotation) % top, axis=1)


def shares(number_of, total, bound, slope, full):
    loads = [(1 << 20) // math.isqrt(grade ** slope) + 1 for grade in range(1, number_of + 1)]
    largest = bound if full else min(bound, max(-(-total // number_of), total * loads[0] // sum(loads)))
    least = 1 if total - largest >= number_of - 1 else 0
    given, spare = [largest] + [least] * (number_of - 1), total - largest - least * (number_of - 1)
    while spare > 0:
        movable = [i for i in range(1, number_of) if given[i] < largest] or [i for i in range(1, number_of) if given[i] < bound]
        whole, left = sum([loads[i] for i in movable]), spare
        for i in movable:
            extra = min(bound - given[i], max(1, left * loads[i] // whole), spare)
            given[i] = given[i] + extra
            spare = spare - extra
    return np.array(given)


def gaussian(key, extent, width, reach, pieces=(), held_as=jnp.bfloat16):
    array = jax.random.normal(key, extent, jnp.float32) * width
    if len(pieces) > 0:
        array = level_of(key, extent, pieces, -0.22, 0.18) * array
    return jnp.clip(array, min=-reach, max=reach).astype(held_as)


def heavy_noise(rng, extent, width, most, split, heavy, kind=jnp.bfloat16):
    values = width * jax.random.normal(rng, extent, jnp.float32)
    if split:
        values = values * level_of(rng, extent, split, -0.22, 0.18)
    return jnp.clip(strengthened(values, jax.random.fold_in(rng, 3), *heavy), -most, most).astype(kind)


def setup_inputs(seed: int = 0) -> dict:
    key_list = jax.random.split(jax.random.key(seed), 8)
    signal = gaussian(key_list[0], (SAMPLES,), 1.0, 6.0, ((0, 128),), jnp.float32)
    weight = jnp.clip(0.25 + 0.75 * jax.random.uniform(key_list[1], (SAMPLES,), jnp.float32) ** level_of(key_list[1], (SAMPLES,), ((0, 128),), -0.2, 0.2), 0.25, 1.0)
    cycle = with_ends(jax.random.randint(key_list[2], (SAMPLES,), 0, CYCLE_DEV), jax.random.fold_in(key_list[2], 1), 0, CYCLE_DEV - 1).astype(jnp.int32)
    phi = with_ends(jax.random.randint(key_list[3], (SAMPLES,), 0, NPHI), jax.random.fold_in(key_list[3], 1), 0, NPHI - 1).astype(jnp.int32)
    psi = with_ends(jax.random.randint(key_list[4], (SAMPLES,), 0, NPSI), jax.random.fold_in(key_list[4], 1), 0, NPSI - 1).astype(jnp.int32)
    owner_keys = jax.random.split(jax.random.fold_in(key_list[5], 1), BLOCKS // BLK_DEV)
    owner_turns = jax.random.permutation(jax.random.fold_in(key_list[5], 3), BLOCKS // BLK_DEV)
    owner = jax.vmap(lambda own, number: deal_out(jax.random.fold_in(key_list[5], 2), own, number, BLK_DEV, N_BLK, 1, CAP, 2))(owner_keys, owner_turns).reshape((BLOCKS, 1))
    wigner = heavy_noise(key_list[6], (NM, NPSI, CYCLES, L), (NPSI * CYCLES) ** -0.5, 0.25, ((0, 16), (1, 8)), (1, 0, 16, 2.0))
    return {"signal": signal, "weight": weight, "cycle": cycle, "phi": phi, "psi": psi, "owner": owner, "wigner": wigner}


def psi_rows(psi_index, length):
    component = jnp.arange(length, dtype=jnp.int32)[:, None]
    middle = length // 2
    frequency = jnp.where(component <= middle, component, component - middle)
    residue = (frequency * psi_index[None, :] % length).astype(jnp.float32)
    angles = residue * jnp.float32(2.0 * math.pi / length)
    return jnp.where(component <= middle, jnp.cos(angles), jnp.sin(angles)) * jnp.float32(1.0 / math.sqrt(length))

def phi_table(length):
    cell_index = jnp.arange(length, dtype=jnp.int32)[:, None]
    column = jnp.arange(length, dtype=jnp.int32)[None, :]
    residue = (column // 2 * cell_index % length).astype(jnp.float32)
    angles = residue * jnp.float32(2.0 * math.pi / length)
    values = jnp.where(column % 2 == 0, jnp.cos(angles), jnp.sin(angles)) * jnp.float32(1.0 / math.sqrt(length))
    return values.astype(jnp.bfloat16)

def reference(signal, weight, cycle, phi, psi, owner, wigner):
    sample_value = signal * weight
    beam_rows = psi_rows(psi, NPSI) * sample_value[None, :]
    beam_rows = lax.optimization_barrier(beam_rows.astype(jnp.bfloat16)).astype(jnp.float32)
    theta = jnp.repeat(owner[:, 0], BLOCK_ROWS) * CYCLE_DEV + cycle
    target = (theta * NPHI + phi).astype(jnp.int32)
    cube = jax.ops.segment_sum(beam_rows.T, target, num_segments=CYCLES * NPHI)
    cube = cube.reshape(CYCLES, NPHI, NPSI).transpose(0, 2, 1).astype(jnp.bfloat16)
    spectra = jnp.dot(cube.reshape(CYCLES * NPSI, NPHI), phi_table(NPHI), preferred_element_type=jnp.float32)
    spectra = spectra.astype(jnp.bfloat16).reshape(CYCLES, NPSI, NM, 2)
    stacked = spectra.transpose(2, 1, 0, 3).reshape(NM, NPSI * CYCLES, 2)

    def one_order(pair):
        table, column = pair
        return jnp.dot(column.T, table.reshape(NPSI * CYCLES, L), preferred_element_type=jnp.float32)
    return lax.map(one_order, (wigner, stacked))
```

```python
import functools
import math

import jax
import jax.numpy as jnp
import numpy as np
from jax import lax
from jax.experimental import pallas as pl
from jax.experimental.pallas import tpu as pltpu
from jax.sharding import PartitionSpec as P

MESH = pl.DeviceIdType.MESH
F32 = jnp.float32
BF16 = jnp.bfloat16
NG = 16
NB = 8
NPSI = 32
NPHI = 2048
CAP = 20
CHUNK = 4
NCH = CAP // CHUNK
ROWS = 16 * NCH
L = 1152


def tables():
    q = np.arange(NPSI)[:, None]
    j = np.arange(NPSI)[None, :]
    psi = np.where(
        q <= 16, np.cos(2 * math.pi * ((q * j) % 32) / 32), np.sin(2 * math.pi * (((q - 16) * j) % 32) / 32)
    ) / math.sqrt(32)
    psi2 = np.einsum("qj,tu,fg->qtfujg", psi, np.eye(2), np.eye(8)).reshape(512, 512)
    f1 = np.arange(64)[:, None]
    r = np.arange(64)[None, :]
    angle = 2 * math.pi * ((r * f1) % 64) / 64
    cs = np.stack([np.cos(angle), np.sin(angle)], axis=1)
    cs = np.repeat(cs[:, :, :, None], 2, axis=3).reshape(64, 256)
    t1 = np.einsum("ab,fn->afbn", np.eye(4), cs).reshape(256, 1024)
    f0 = np.arange(32)[:, None]
    turn = 2 * math.pi * (r * f0) / 2048
    tr, ti = np.cos(turn) / math.sqrt(NPHI), np.sin(turn) / math.sqrt(NPHI)
    a = np.stack([tr, ti], axis=2).reshape(4, 8, 128)
    b = np.stack([-ti, tr], axis=2).reshape(4, 8, 128)
    tw = np.stack([a, b], axis=1)
    blk = np.arange(NG)[:, None]
    outer = 2 * math.pi * ((blk * np.arange(32)[None, :]) % 32) / 32
    cos, sin = np.cos(outer).reshape(NG, 4, 8), np.sin(outer).reshape(NG, 4, 8)
    both = np.stack([cos, sin], axis=2)
    d2 = np.einsum("bayf,st->bsaytf", both, np.eye(8)).reshape(128, 512)
    row = np.arange(128)
    b_, q_, t_ = row // 8, row // 2 % 4, row % 2
    e = np.zeros((128, 128))
    e[row, q_ * 32 + 2 * b_ + t_] = 1
    return (
        jnp.asarray(psi2, BF16),
        jnp.asarray(t1, BF16),
        jnp.asarray(tw, F32),
        jnp.asarray(d2, BF16),
        jnp.asarray(e, BF16),
    )


def send_kernel(signal, weight, cycle, phi, psi, owner, out, data, sendbuf, send_sem, recv_sem):
    me, row = lax.axis_index("blk"), lax.axis_index("beam")
    barrier = pltpu.get_barrier_semaphore()

    def greet(i, c):
        pl.semaphore_signal(barrier, inc=1, device_id=(lax.rem(me + i, NG), row), device_id_type=MESH)
        return c

    lax.fori_loop(1, NG, greet, 0)
    value = signal[...] * weight[...]
    zero = jnp.zeros_like(value)
    cyc = cycle[...]
    cell = phi[...]
    data[0:128] = jnp.where(cyc == 0, value, zero).astype(BF16)
    data[128:256] = jnp.where(cyc == 0, zero, value).astype(BF16)
    data[256:384] = (psi[...] * 8 + (cell & 7) + 1).astype(F32).astype(BF16)
    data[384:512] = (((cell >> 3) & 3) * 64 + (cell >> 5) + 1).astype(F32).astype(BF16)
    own = owner[...]
    hit = lax.broadcasted_iota(jnp.int32, (NG, 128), 0) == own
    upper = lax.broadcasted_iota(jnp.int32, (128, 128), 0) < lax.broadcasted_iota(jnp.int32, (128, 128), 1)
    before = jnp.dot(
        jnp.where(hit, 1.0, 0.0).astype(BF16), jnp.where(upper, 1.0, 0.0).astype(BF16), preferred_element_type=F32
    )
    within = jnp.sum(jnp.where(hit, before, 0.0), axis=0, keepdims=True).astype(jnp.int32)
    key = own * 1024 + within
    key = jnp.concatenate([key, key + 32, key + 64, key + 96], axis=1)
    at = lax.broadcasted_iota(jnp.int32, (ROWS, 512), 0)
    base = ((at >> 4) * CHUNK + (at & 3)) + ((at >> 2) & 3) * 32
    pl.semaphore_wait(barrier, NG - 1)

    def copy(g):
        return pltpu.make_async_remote_copy(
            src_ref=sendbuf.at[g],
            dst_ref=out.at[me],
            send_sem=send_sem.at[g],
            recv_sem=recv_sem.at[me],
            device_id=(g, row),
            device_id_type=MESH,
        )

    def arrival(g):
        return pltpu.make_async_remote_copy(
            src_ref=sendbuf.at[g],
            dst_ref=out.at[g],
            send_sem=send_sem.at[g],
            recv_sem=recv_sem.at[g],
            device_id=(g, row),
            device_id_type=MESH,
        )

    def rows_of(g):
        chosen = jnp.where(base == key - g * 1024, 1.0, 0.0).astype(BF16)
        return jnp.dot(chosen, data[...], preferred_element_type=F32).astype(BF16)

    def send(i, c):
        g = lax.rem(me + i, NG)
        sendbuf[g] = rows_of(g)
        copy(g).start()
        return c

    lax.fori_loop(1, NG, send, 0)
    out[me] = rows_of(me)

    def settle(i, c):
        g = lax.rem(me + i, NG)
        copy(g).wait_send()
        arrival(g).wait_recv()
        return c

    lax.fori_loop(1, NG, settle, 0)


def bin_kernel(got, psi2, cube, acc, flag_v, flag_s, sem):
    flag_v[...] = got[...].astype(F32)[:, 8, :].astype(jnp.int32)
    move = pltpu.make_async_copy(flag_v, flag_s, sem)
    move.start()
    acc[...] = jnp.zeros_like(acc)
    move.wait()
    cells = (lax.broadcasted_iota(jnp.int32, (256, 128), 0) + 1).astype(F32).astype(BF16)
    one, zero = jnp.ones((256, 128), BF16), jnp.zeros((256, 128), BF16)

    def step(n, c):
        @pl.when(flag_s[n, 0] > 0)
        def _():
            tile = got[n]
            low, high, right = [], [], []
            for i in range(CHUNK):
                at = tile[8 + i : 9 + i] == cells
                low.append(jnp.where(at, jnp.broadcast_to(tile[i : i + 1], (256, 128)), zero))
                high.append(jnp.where(at, jnp.broadcast_to(tile[4 + i : 5 + i], (256, 128)), zero))
                right.append(jnp.where(tile[12 + i : 13 + i] == cells, one, zero))
            left = jnp.concatenate([jnp.concatenate(low, axis=1), jnp.concatenate(high, axis=1)], axis=0)
            acc[...] += lax.dot_general(
                left, jnp.concatenate(right, axis=1), (((1,), (1,)), ((), ())), preferred_element_type=F32
            )

        return c

    lax.fori_loop(0, NG * NCH, step, 0)
    cube[...] = jnp.dot(psi2[...], acc[...].astype(BF16), preferred_element_type=F32).astype(BF16)


def tail_kernel(
    cube, t1, tw, d2, perm, wigner, out,
    wig, got_a, mix, spec, got_c, coef, send_e, got_e,
    wig_sem, send_a, recv_a, send_c, recv_c, send_sem_e, recv_sem_e,
):
    blk, beam = lax.axis_index("blk"), lax.axis_index("beam")
    barrier = pltpu.get_barrier_semaphore()

    def load(e):
        rows = pl.ds(pl.multiple_of(e * 1024, 1024), 1024)
        return pltpu.make_async_copy(wigner.at[rows], wig.at[rows], wig_sem.at[e])

    def greet_blk(i, c):
        pl.semaphore_signal(barrier, inc=1, device_id=(lax.rem(blk + i, NG), beam), device_id_type=MESH)
        return c

    def greet_beam(i, c):
        pl.semaphore_signal(barrier, inc=1, device_id=(blk, lax.rem(beam + i, NB)), device_id_type=MESH)
        return c

    lax.fori_loop(1, NB, greet_beam, 0)
    lax.fori_loop(1, NG, greet_blk, 0)
    pl.semaphore_wait(barrier, NG + NB - 2)

    def copy_a(e, slot):
        return pltpu.make_async_remote_copy(
            src_ref=cube.at[pl.ds(pl.multiple_of(e * 64, 64), 64)],
            dst_ref=got_a.at[slot],
            send_sem=send_a.at[e],
            recv_sem=recv_a.at[slot],
            device_id=(blk, e),
            device_id_type=MESH,
        )

    def start_a(i, c):
        copy_a(lax.rem(beam + i, NB), beam).start()
        return c

    lax.fori_loop(1, NB, start_a, 0)

    def start_load(i, c):
        load(lax.rem(beam + i, NB)).start()
        return c

    lax.fori_loop(1, NB + 1, start_load, 0)
    mine = cube[pl.ds(pl.multiple_of(beam * 64, 64), 64), :].astype(F32)

    def settle_a(i, total):
        e = lax.rem(beam + i, NB)
        copy_a(e, e).wait_recv()
        return total + got_a[e].astype(F32)

    x = lax.fori_loop(1, NB, settle_a, mine).astype(BF16)
    pq = jnp.dot(x, t1[...], preferred_element_type=F32)
    for a in range(4):
        p = pq[:, a * 256 : a * 256 + 128].reshape(8, 8, 128)
        q = pq[:, a * 256 + 128 : a * 256 + 256].reshape(8, 8, 128)
        ta, tb = tw[a, 0][None], tw[a, 1][None]
        mix[a * 128 : a * 128 + 64] = (p * ta + q * tb).reshape(64, 128).astype(BF16)
        mix[a * 128 + 64 : a * 128 + 128] = (p * tb - q * ta).reshape(64, 128).astype(BF16)
    spec[...] = jnp.dot(d2[...], mix[...], preferred_element_type=F32).reshape(NG, 8, 128)

    def copy_c(g, slot):
        return pltpu.make_async_remote_copy(
            src_ref=spec.at[g],
            dst_ref=got_c.at[slot],
            send_sem=send_c.at[g],
            recv_sem=recv_c.at[slot],
            device_id=(g, beam),
            device_id_type=MESH,
        )

    def start_c(i, c):
        copy_c(lax.rem(blk + i, NG), blk).start()
        return c

    lax.fori_loop(1, NG, start_c, 0)
    got_c[blk] = spec[blk]

    def settle_c(i, c):
        g = lax.rem(blk + i, NG)
        copy_c(g, g).wait_recv()
        return c

    lax.fori_loop(1, NG, settle_c, 0)
    coef[...] = lax.dot_general(
        got_c[...].reshape(128, 128).astype(BF16), perm[...], (((0,), (0,)), ((), ())), preferred_element_type=F32
    ).astype(BF16)
    diagonal = (lax.broadcasted_iota(jnp.int32, (16, 1024), 0) >> 1) == (
        lax.broadcasted_iota(jnp.int32, (16, 1024), 1) >> 7
    )

    def copy_e(e, slot):
        return pltpu.make_async_remote_copy(
            src_ref=send_e.at[e],
            dst_ref=got_e.at[slot],
            send_sem=send_sem_e.at[e],
            recv_sem=recv_sem_e.at[slot],
            device_id=(blk, e),
            device_id_type=MESH,
        )

    def contract(i, c):
        e = lax.rem(beam + i, NB)
        load(e).wait()
        rows = coef[pl.ds(pl.multiple_of(e * 16, 16), 16), :].astype(F32)
        left = jnp.where(diagonal, jnp.concatenate([rows] * 8, axis=1), 0.0).astype(BF16)
        part = jnp.dot(left, wig[pl.ds(pl.multiple_of(e * 1024, 1024), 1024), :], preferred_element_type=F32)

        @pl.when(i < NB)
        def _():
            send_e[e] = part.astype(BF16)
            copy_e(e, beam).start()

        @pl.when(i == NB)
        def _():
            out[...] = part

        return c

    lax.fori_loop(1, NB + 1, contract, 0)

    def settle_e(i, c):
        e = lax.rem(beam + i, NB)
        copy_e(e, e).wait_recv()
        out[...] += got_e[e].astype(F32)
        return c

    lax.fori_loop(1, NB, settle_e, 0)

    def sent_beam(i, c):
        e = lax.rem(beam + i, NB)
        copy_a(e, e).wait_send()
        copy_e(e, e).wait_send()
        return c

    def sent_blk(i, c):
        g = lax.rem(blk + i, NG)
        copy_c(g, g).wait_send()
        return c

    lax.fori_loop(1, NB, sent_beam, 0)
    lax.fori_loop(1, NG, sent_blk, 0)


VMEM = functools.partial(pl.BlockSpec, memory_space=pltpu.VMEM)


def shards(signal, weight, cycle, phi, psi, owner, wigner):
    psi2, t1, tw, d2, perm = tables()
    block = lambda x: x.reshape(128, 128)
    dma = pltpu.SemaphoreType.DMA
    got = pl.pallas_call(
        send_kernel,
        out_shape=jax.ShapeDtypeStruct((NG, ROWS, 128), BF16),
        in_specs=[VMEM()] * 6,
        out_specs=VMEM(),
        scratch_shapes=[
            pltpu.VMEM((512, 128), BF16),
            pltpu.VMEM((NG, ROWS, 128), BF16),
            dma((NG,)),
            dma((NG,)),
        ],
        compiler_params=pltpu.CompilerParams(
            collective_id=0, has_side_effects=True, vmem_limit_bytes=16 * 2**20
        ),
        name="send_samples",
    )(block(signal), block(weight), block(cycle), block(phi), block(psi), owner.reshape(1, 128))
    cube = pl.pallas_call(
        bin_kernel,
        out_shape=jax.ShapeDtypeStruct((512, 256), BF16),
        in_specs=[VMEM()] * 2,
        out_specs=VMEM(),
        scratch_shapes=[
            pltpu.VMEM((512, 256), F32),
            pltpu.VMEM((NG * NCH, 128), jnp.int32),
            pltpu.SMEM((NG * NCH, 128), jnp.int32),
            dma,
        ],
        compiler_params=pltpu.CompilerParams(vmem_limit_bytes=24 * 2**20),
        name="bin_samples",
    )(got.reshape(NG * NCH, 16, 128), psi2)
    alm = pl.pallas_call(
        tail_kernel,
        out_shape=jax.ShapeDtypeStruct((16, L), F32),
        in_specs=[VMEM()] * 5 + [pl.BlockSpec(memory_space=pl.ANY)],
        out_specs=VMEM(),
        scratch_shapes=[
            pltpu.VMEM((64 * 128, L), BF16),
            pltpu.VMEM((NB, 64, 256), BF16),
            pltpu.VMEM((512, 128), BF16),
            pltpu.VMEM((NG, 8, 128), F32),
            pltpu.VMEM((NG, 8, 128), F32),
            pltpu.VMEM((128, 128), BF16),
            pltpu.VMEM((NB, 16, L), BF16),
            pltpu.VMEM((NB, 16, L), BF16),
            dma((NB,)),
            dma((NB,)),
            dma((NB,)),
            dma((NG,)),
            dma((NG,)),
            dma((NB,)),
            dma((NB,)),
        ],
        compiler_params=pltpu.CompilerParams(
            collective_id=1, has_side_effects=True, vmem_limit_bytes=40 * 2**20
        ),
        name="sky_coefficients",
    )(cube, t1, tw, d2, perm, wigner.reshape(64 * 128, L))
    return alm.reshape(8, 2, L)


def solution(mesh):
    return jax.shard_map(
        shards,
        mesh=mesh,
        in_specs=(
            P(("blk", "beam")),
            P(("blk", "beam")),
            P(("blk", "beam")),
            P(("blk", "beam")),
            P(("blk", "beam")),
            P(("blk", "beam"), None),
            P("blk", "beam", None, None),
        ),
        out_specs=P(("blk", "beam"), None, None),
        check_vma=False,
    )
```

```python
import math

import jax
import jax.numpy as jnp
import numpy as np
from jax import lax
from jax.experimental import pallas as pl
from jax.experimental.pallas import tpu as pltpu
from jax.sharding import PartitionSpec as P

MESH = pl.DeviceIdType.MESH
F32 = jnp.float32
BF16 = jnp.bfloat16
NG = 16
NB = 8
NPSI = 32
NPHI = 2048
CAP = 20
CHUNK = 4
NCH = CAP // CHUNK
ROWS = 16 * NCH
L = 1152


def tables():
    q = np.arange(NPSI)[:, None]
    j = np.arange(NPSI)[None, :]
    psi = np.where(
        q <= 16, np.cos(2 * math.pi * ((q * j) % 32) / 32), np.sin(2 * math.pi * (((q - 16) * j) % 32) / 32)
    ) / math.sqrt(32)
    psi2 = np.einsum("qj,tu,fg->qtfujg", psi, np.eye(2), np.eye(8)).reshape(512, 512)
    f1 = np.arange(64)[:, None]
    r = np.arange(64)[None, :]
    angle = 2 * math.pi * ((r * f1) % 64) / 64
    cs = np.stack([np.cos(angle), np.sin(angle)], axis=1)
    cs = np.repeat(cs[:, :, :, None], 2, axis=3).reshape(64, 256)
    t1 = np.einsum("ab,fn->afbn", np.eye(4), cs).reshape(256, 1024)
    f0 = np.arange(32)[:, None]
    turn = 2 * math.pi * (r * f0) / 2048
    tr, ti = np.cos(turn) / math.sqrt(NPHI), np.sin(turn) / math.sqrt(NPHI)
    a = np.stack([tr, ti], axis=2).reshape(4, 8, 128)
    b = np.stack([-ti, tr], axis=2).reshape(4, 8, 128)
    tw = np.stack([a, b], axis=1)
    blk = np.arange(NG)[:, None]
    outer = 2 * math.pi * ((blk * np.arange(32)[None, :]) % 32) / 32
    cos, sin = np.cos(outer).reshape(NG, 4, 8), np.sin(outer).reshape(NG, 4, 8)
    both = np.stack([cos, sin], axis=2)
    d2 = np.einsum("bayf,st->bsaytf", both, np.eye(8)).reshape(128, 512)
    row = np.arange(128)
    b_, q_, t_ = row // 8, row // 2 % 4, row % 2
    e = np.zeros((128, 128))
    e[row, q_ * 32 + 2 * b_ + t_] = 1
    return (
        jnp.asarray(psi2, BF16),
        jnp.asarray(t1, BF16),
        jnp.asarray(tw, F32),
        jnp.asarray(d2, BF16),
        jnp.asarray(e, BF16),
    )


def kernel(
    signal, weight, cycle, phi, psi, owner, psi2, t1, tw, d2, perm, wigner, out,
    signal_v, weight_v, cycle_v, phi_v, psi_v, owner_v, psi2_v, t1_v, tw_v, d2_v, perm_v, wig,
    data, sendbuf, got, acc, dense, cube, got_a, mix, spec, got_c, coef, send_e, got_e,
    in_sem, wig_sem, send_s, recv_s, send_a, recv_a, send_c, recv_c, send_sem_e, recv_sem_e,
):
    blk, beam = lax.axis_index("blk"), lax.axis_index("beam")
    barrier = pltpu.get_barrier_semaphore()

    sources = (signal, weight, cycle, phi, psi, owner, psi2, t1, tw, d2, perm)
    places = (signal_v, weight_v, cycle_v, phi_v, psi_v, owner_v, psi2_v, t1_v, tw_v, d2_v, perm_v)
    fetches = [pltpu.make_async_copy(a, b, in_sem.at[n]) for n, (a, b) in enumerate(zip(sources, places))]
    for fetch in fetches:
        fetch.start()

    def greet_blk(i, c):
        pl.semaphore_signal(barrier, inc=1, device_id=(lax.rem(blk + i, NG), beam), device_id_type=MESH)
        return c

    def greet_beam(i, c):
        pl.semaphore_signal(barrier, inc=1, device_id=(blk, lax.rem(beam + i, NB)), device_id_type=MESH)
        return c

    lax.fori_loop(1, NG, greet_blk, 0)
    lax.fori_loop(1, NB, greet_beam, 0)

    def load(e):
        rows = pl.ds(pl.multiple_of(e * 1024, 1024), 1024)
        return pltpu.make_async_copy(wigner.at[rows], wig.at[rows], wig_sem.at[e])

    def start_load(i, c):
        load(lax.rem(beam + i, NB)).start()
        return c

    lax.fori_loop(1, NB + 1, start_load, 0)

    for fetch in fetches[:6]:
        fetch.wait()
    value = signal_v[...] * weight_v[...]
    zero = jnp.zeros_like(value)
    cyc = cycle_v[...]
    cell = phi_v[...]
    data[0:128] = jnp.where(cyc == 0, value, zero).astype(BF16)
    data[128:256] = jnp.where(cyc == 0, zero, value).astype(BF16)
    data[256:384] = (psi_v[...] * 8 + (cell & 7) + 1).astype(F32).astype(BF16)
    data[384:512] = (((cell >> 3) & 3) * 64 + (cell >> 5) + 1).astype(F32).astype(BF16)
    own = owner_v[...]
    hit = lax.broadcasted_iota(jnp.int32, (NG, 128), 0) == own
    upper = lax.broadcasted_iota(jnp.int32, (128, 128), 0) < lax.broadcasted_iota(jnp.int32, (128, 128), 1)
    before = jnp.dot(
        jnp.where(hit, 1.0, 0.0).astype(BF16), jnp.where(upper, 1.0, 0.0).astype(BF16), preferred_element_type=F32
    )
    within = jnp.sum(jnp.where(hit, before, 0.0), axis=0, keepdims=True).astype(jnp.int32)
    key = own * 1024 + within
    key = jnp.concatenate([key, key + 32, key + 64, key + 96], axis=1)
    at = lax.broadcasted_iota(jnp.int32, (ROWS, 512), 0)
    base = ((at >> 4) * CHUNK + (at & 3)) + ((at >> 2) & 3) * 32

    def copy_s(g, slot):
        return pltpu.make_async_remote_copy(
            src_ref=sendbuf.at[g],
            dst_ref=got.at[slot],
            send_sem=send_s.at[g],
            recv_sem=recv_s.at[slot],
            device_id=(g, beam),
            device_id_type=MESH,
        )

    def rows_of(first, count):
        keys = [base + lax.rem(blk + first + n, NG) * 1024 for n in range(count)]
        chosen = jnp.where(jnp.concatenate(keys, axis=0) == key, 1.0, 0.0).astype(BF16)
        return jnp.dot(chosen, data[...], preferred_element_type=F32).astype(BF16)

    pl.semaphore_wait(barrier, NG + NB - 2)

    def send(i, c):
        rows = rows_of(i * 3 + 1, 3)
        for n in range(3):
            g = lax.rem(blk + i * 3 + 1 + n, NG)
            sendbuf[g] = rows[n * ROWS : (n + 1) * ROWS]
            copy_s(g, blk).start()
        return c

    lax.fori_loop(0, 5, send, 0)
    got[blk] = rows_of(0, 1)

    cells = (lax.broadcasted_iota(jnp.int32, (256, 128), 0) + 1).astype(F32).astype(BF16)
    one, nil = jnp.ones((256, 128), BF16), jnp.zeros((256, 128), BF16)

    def bin_two(first, second):
        low, high, right = [], [], []
        for source in (first, second):
            for n in range(NCH):
                tile = got[source, 16 * n : 16 * n + 16]
                for i in range(CHUNK):
                    same = tile[8 + i : 9 + i] == cells
                    low.append(jnp.where(same, jnp.broadcast_to(tile[i : i + 1], (256, 128)), nil))
                    high.append(jnp.where(same, jnp.broadcast_to(tile[4 + i : 5 + i], (256, 128)), nil))
                    right.append(jnp.where(tile[12 + i : 13 + i] == cells, one, nil))
        left = jnp.concatenate([jnp.concatenate(low, axis=1), jnp.concatenate(high, axis=1)], axis=0)
        return lax.dot_general(
            left, jnp.concatenate(right, axis=1), (((1,), (1,)), ((), ())), preferred_element_type=F32
        )

    acc[...] = jnp.zeros_like(acc)

    def bins(i, c):
        first = lax.rem(blk + NG - 2 * i, NG)
        second = lax.rem(blk + NG - 2 * i - 1, NG)

        @pl.when(i > 0)
        def _():
            copy_s(first, first).wait_recv()

        copy_s(second, second).wait_recv()
        acc[...] += bin_two(first, second)
        return c

    lax.fori_loop(0, NG // 2, bins, 0)
    dense[...] = acc[...].astype(BF16)
    for fetch in fetches[6:]:
        fetch.wait()

    def copy_a(e, slot):
        return pltpu.make_async_remote_copy(
            src_ref=cube.at[e],
            dst_ref=got_a.at[slot],
            send_sem=send_a.at[e],
            recv_sem=recv_a.at[slot],
            device_id=(blk, e),
            device_id_type=MESH,
        )

    def share(e):
        rows = psi2_v[pl.ds(pl.multiple_of(e * 64, 64), 64), :]
        return jnp.dot(rows, dense[...], preferred_element_type=F32)

    def start_a(i, c):
        e = lax.rem(beam + i, NB)
        cube[e] = share(e).astype(BF16)
        copy_a(e, beam).start()
        return c

    lax.fori_loop(1, NB, start_a, 0)

    def settle_a(i, total):
        e = lax.rem(beam + NB - i, NB)
        copy_a(e, e).wait_recv()
        return total + got_a[e].astype(F32)

    x = lax.fori_loop(1, NB, settle_a, share(beam)).astype(BF16)
    pq = jnp.dot(x, t1_v[...], preferred_element_type=F32)
    for a in range(4):
        p = pq[:, a * 256 : a * 256 + 128].reshape(8, 8, 128)
        q = pq[:, a * 256 + 128 : a * 256 + 256].reshape(8, 8, 128)
        ta, tb = tw_v[a, 0][None], tw_v[a, 1][None]
        mix[a * 128 : a * 128 + 64] = (p * ta + q * tb).reshape(64, 128).astype(BF16)
        mix[a * 128 + 64 : a * 128 + 128] = (p * tb - q * ta).reshape(64, 128).astype(BF16)
    spec[...] = jnp.dot(d2_v[...], mix[...], preferred_element_type=F32).reshape(NG, 8, 128)

    def copy_c(g, slot):
        return pltpu.make_async_remote_copy(
            src_ref=spec.at[g],
            dst_ref=got_c.at[slot],
            send_sem=send_c.at[g],
            recv_sem=recv_c.at[slot],
            device_id=(g, beam),
            device_id_type=MESH,
        )

    def start_c(i, c):
        copy_c(lax.rem(blk + i, NG), blk).start()
        return c

    lax.fori_loop(1, NG, start_c, 0)
    got_c[blk] = spec[blk]

    def settle_c(i, c):
        g = lax.rem(blk + NG - i, NG)
        copy_c(g, g).wait_recv()
        return c

    lax.fori_loop(1, NG, settle_c, 0)
    coef[...] = lax.dot_general(
        got_c[...].reshape(128, 128).astype(BF16), perm_v[...], (((0,), (0,)), ((), ())), preferred_element_type=F32
    ).astype(BF16)
    diagonal = (lax.broadcasted_iota(jnp.int32, (16, 1024), 0) >> 1) == (
        lax.broadcasted_iota(jnp.int32, (16, 1024), 1) >> 7
    )

    def copy_e(e, slot):
        return pltpu.make_async_remote_copy(
            src_ref=send_e.at[e],
            dst_ref=got_e.at[slot],
            send_sem=send_sem_e.at[e],
            recv_sem=recv_sem_e.at[slot],
            device_id=(blk, e),
            device_id_type=MESH,
        )

    def contract(i, c):
        e = lax.rem(beam + i, NB)
        load(e).wait()
        rows = coef[pl.ds(pl.multiple_of(e * 16, 16), 16), :].astype(F32)
        left = jnp.where(diagonal, jnp.concatenate([rows] * 8, axis=1), 0.0).astype(BF16)
        part = jnp.dot(left, wig[pl.ds(pl.multiple_of(e * 1024, 1024), 1024), :], preferred_element_type=F32)

        @pl.when(i < NB)
        def _():
            send_e[e] = part.astype(BF16)
            copy_e(e, beam).start()

        @pl.when(i == NB)
        def _():
            out[...] = part

        return c

    lax.fori_loop(1, NB + 1, contract, 0)

    def settle_e(i, c):
        e = lax.rem(beam + NB - i, NB)
        copy_e(e, e).wait_recv()
        out[...] += got_e[e].astype(F32)
        return c

    lax.fori_loop(1, NB, settle_e, 0)

    def sent_beam(i, c):
        e = lax.rem(beam + i, NB)
        copy_a(e, e).wait_send()
        copy_e(e, e).wait_send()
        return c

    def sent_blk(i, c):
        g = lax.rem(blk + i, NG)
        copy_s(g, g).wait_send()
        copy_c(g, g).wait_send()
        return c

    lax.fori_loop(1, NB, sent_beam, 0)
    lax.fori_loop(1, NG, sent_blk, 0)


ANY = pl.BlockSpec(memory_space=pl.ANY)


def shards(signal, weight, cycle, phi, psi, owner, wigner):
    block = lambda x: x.reshape(128, 128)
    dma = pltpu.SemaphoreType.DMA
    operands = (
        block(signal),
        block(weight),
        block(cycle),
        block(phi),
        block(psi),
        owner.reshape(1, 128),
        *tables(),
        wigner.reshape(64 * 128, L),
    )
    alm = pl.pallas_call(
        kernel,
        out_shape=jax.ShapeDtypeStruct((16, L), F32),
        in_specs=[ANY] * len(operands),
        out_specs=pl.BlockSpec(memory_space=pltpu.VMEM),
        scratch_shapes=[
            *(pltpu.VMEM(x.shape, x.dtype) for x in operands),
            pltpu.VMEM((512, 128), BF16),
            pltpu.VMEM((NG, ROWS, 128), BF16),
            pltpu.VMEM((NG, ROWS, 128), BF16),
            pltpu.VMEM((512, 256), F32),
            pltpu.VMEM((512, 256), BF16),
            pltpu.VMEM((NB, 64, 256), BF16),
            pltpu.VMEM((NB, 64, 256), BF16),
            pltpu.VMEM((512, 128), BF16),
            pltpu.VMEM((NG, 8, 128), F32),
            pltpu.VMEM((NG, 8, 128), F32),
            pltpu.VMEM((128, 128), BF16),
            pltpu.VMEM((NB, 16, L), BF16),
            pltpu.VMEM((NB, 16, L), BF16),
            dma((11,)),
            dma((NB,)),
            dma((NG,)),
            dma((NG,)),
            dma((NB,)),
            dma((NB,)),
            dma((NG,)),
            dma((NG,)),
            dma((NB,)),
            dma((NB,)),
        ],
        compiler_params=pltpu.CompilerParams(
            collective_id=0, has_side_effects=True, vmem_limit_bytes=56 * 2**20
        ),
        name="sky_coefficients",
    )(*operands)
    return alm.reshape(8, 2, L)


def solution(mesh):
    return jax.shard_map(
        shards,
        mesh=mesh,
        in_specs=(
            P(("blk", "beam")),
            P(("blk", "beam")),
            P(("blk", "beam")),
            P(("blk", "beam")),
            P(("blk", "beam")),
            P(("blk", "beam"), None),
            P("blk", "beam", None, None),
        ),
        out_specs=P(("blk", "beam"), None, None),
        check_vma=False,
    )
```

```python
import math

import jax
import jax.numpy as jnp
import numpy as np
from jax import lax
from jax.experimental import pallas as pl
from jax.experimental.pallas import tpu as pltpu
from jax.sharding import PartitionSpec as P

MESH = pl.DeviceIdType.MESH
F32 = jnp.float32
BF16 = jnp.bfloat16
NG = 16
NB = 8
NPSI = 32
NPHI = 2048
CAP = 20
CHUNK = 4
NCH = CAP // CHUNK
ROWS = 16 * NCH
L = 1152


def tables():
    q = np.arange(NPSI)[:, None]
    j = np.arange(NPSI)[None, :]
    psi = np.where(
        q <= 16, np.cos(2 * math.pi * ((q * j) % 32) / 32), np.sin(2 * math.pi * (((q - 16) * j) % 32) / 32)
    ) / math.sqrt(32)
    psi2 = np.einsum("qj,tu,fg->qtfujg", psi, np.eye(2), np.eye(8)).reshape(512, 512)
    f1 = np.arange(64)[:, None]
    r = np.arange(64)[None, :]
    angle = 2 * math.pi * ((r * f1) % 64) / 64
    cs = np.stack([np.cos(angle), np.sin(angle)], axis=1)
    cs = np.repeat(cs[:, :, :, None], 2, axis=3).reshape(64, 256)
    t1 = np.einsum("ab,fn->afbn", np.eye(4), cs).reshape(256, 1024)
    f0 = np.arange(32)[:, None]
    turn = 2 * math.pi * (r * f0) / 2048
    tr, ti = np.cos(turn) / math.sqrt(NPHI), np.sin(turn) / math.sqrt(NPHI)
    a = np.stack([tr, ti], axis=2).reshape(4, 8, 128)
    b = np.stack([-ti, tr], axis=2).reshape(4, 8, 128)
    tw = np.stack([a, b], axis=1)
    blk = np.arange(NG)[:, None]
    outer = 2 * math.pi * ((blk * np.arange(32)[None, :]) % 32) / 32
    cos, sin = np.cos(outer).reshape(NG, 4, 8), np.sin(outer).reshape(NG, 4, 8)
    both = np.stack([cos, sin], axis=2)
    d2 = np.einsum("bayf,st->bsaytf", both, np.eye(8)).reshape(128, 512)
    row = np.arange(128)
    b_, q_, t_ = row // 8, row // 2 % 4, row % 2
    e = np.zeros((128, 128))
    e[row, q_ * 32 + 2 * b_ + t_] = 1
    return (
        jnp.asarray(psi2, BF16),
        jnp.asarray(t1, BF16),
        jnp.asarray(tw, F32),
        jnp.asarray(d2, BF16),
        jnp.asarray(e, BF16),
    )


def kernel(
    signal, weight, cycle, phi, psi, owner, psi2, t1, tw, d2, perm, wigner, out,
    signal_v, weight_v, cycle_v, phi_v, psi_v, owner_v, psi2_v, t1_v, tw_v, d2_v, perm_v, wig,
    data, sendbuf, got, acc, dense, cube, got_a, mix, spec, got_c, coef, send_e, got_e,
    in_sem, wig_sem, send_s, recv_s, send_a, recv_a, send_c, recv_c, send_sem_e, recv_sem_e,
):
    blk, beam = lax.axis_index("blk"), lax.axis_index("beam")
    barrier = pltpu.get_barrier_semaphore()

    sources = (signal, weight, cycle, phi, psi, owner, psi2, t1, tw, d2, perm)
    places = (signal_v, weight_v, cycle_v, phi_v, psi_v, owner_v, psi2_v, t1_v, tw_v, d2_v, perm_v)
    fetches = [pltpu.make_async_copy(a, b, in_sem.at[n]) for n, (a, b) in enumerate(zip(sources, places))]
    for fetch in fetches[5::-1]:
        fetch.start()

    def greet_blk(i, c):
        pl.semaphore_signal(barrier, inc=1, device_id=(lax.rem(blk + i, NG), beam), device_id_type=MESH)
        return c

    def greet_beam(i, c):
        pl.semaphore_signal(barrier, inc=1, device_id=(blk, lax.rem(beam + i, NB)), device_id_type=MESH)
        return c

    lax.fori_loop(1, NG, greet_blk, 0)
    lax.fori_loop(1, NB, greet_beam, 0)

    def load(e):
        rows = pl.ds(pl.multiple_of(e * 1024, 1024), 1024)
        return pltpu.make_async_copy(wigner.at[rows], wig.at[rows], wig_sem.at[e])

    def start_load(i, c):
        load(lax.rem(beam + i, NB)).start()
        return c

    for fetch in fetches[:6]:
        fetch.wait()
    value = signal_v[...] * weight_v[...]
    zero = jnp.zeros_like(value)
    cyc = cycle_v[...]
    cell = phi_v[...]
    data[0:128] = jnp.where(cyc == 0, value, zero).astype(BF16)
    data[128:256] = jnp.where(cyc == 0, zero, value).astype(BF16)
    data[256:384] = (psi_v[...] * 8 + (cell & 7) + 1).astype(F32).astype(BF16)
    data[384:512] = (((cell >> 3) & 3) * 64 + (cell >> 5) + 1).astype(F32).astype(BF16)
    own = owner_v[...]
    hit = lax.broadcasted_iota(jnp.int32, (NG, 128), 0) == own
    upper = lax.broadcasted_iota(jnp.int32, (128, 128), 0) < lax.broadcasted_iota(jnp.int32, (128, 128), 1)
    before = jnp.dot(
        jnp.where(hit, 1.0, 0.0).astype(BF16), jnp.where(upper, 1.0, 0.0).astype(BF16), preferred_element_type=F32
    )
    within = jnp.sum(jnp.where(hit, before, 0.0), axis=0, keepdims=True).astype(jnp.int32)
    key = own * 1024 + within
    key = jnp.concatenate([key, key + 32, key + 64, key + 96], axis=1)
    at = lax.broadcasted_iota(jnp.int32, (ROWS, 512), 0)
    base = ((at >> 4) * CHUNK + (at & 3)) + ((at >> 2) & 3) * 32

    def copy_s(g, slot):
        return pltpu.make_async_remote_copy(
            src_ref=sendbuf.at[g],
            dst_ref=got.at[slot],
            send_sem=send_s.at[g],
            recv_sem=recv_s.at[slot],
            device_id=(g, beam),
            device_id_type=MESH,
        )

    def rows_of(i, c):
        chosen = jnp.concatenate([base + (4 * i + n) * 1024 for n in range(4)], axis=0) == key
        rows = jnp.dot(jnp.where(chosen, 1.0, 0.0).astype(BF16), data[...], preferred_element_type=F32)
        sendbuf[pl.ds(4 * i, 4)] = rows.astype(BF16).reshape(4, ROWS, 128)
        return c

    lax.fori_loop(0, NG // 4, rows_of, 0)
    pl.semaphore_wait(barrier, NG + NB - 2)

    def send(i, c):
        copy_s(lax.rem(blk + i, NG), blk).start()
        return c

    lax.fori_loop(1, NG, send, 0)
    got[blk] = sendbuf[blk]
    for fetch in fetches[6:]:
        fetch.start()
    lax.fori_loop(1, NB + 1, start_load, 0)

    cells = (lax.broadcasted_iota(jnp.int32, (256, 128), 0) + 1).astype(F32).astype(BF16)
    one, nil = jnp.ones((256, 128), BF16), jnp.zeros((256, 128), BF16)

    def bin_two(first, second):
        low, high, right = [], [], []
        for source in (first, second):
            for n in range(NCH):
                tile = got[source, 16 * n : 16 * n + 16]
                for i in range(CHUNK):
                    same = tile[8 + i : 9 + i] == cells
                    low.append(jnp.where(same, jnp.broadcast_to(tile[i : i + 1], (256, 128)), nil))
                    high.append(jnp.where(same, jnp.broadcast_to(tile[4 + i : 5 + i], (256, 128)), nil))
                    right.append(jnp.where(tile[12 + i : 13 + i] == cells, one, nil))
        left = jnp.concatenate([jnp.concatenate(low, axis=1), jnp.concatenate(high, axis=1)], axis=0)
        return lax.dot_general(
            left, jnp.concatenate(right, axis=1), (((1,), (1,)), ((), ())), preferred_element_type=F32
        )

    acc[...] = jnp.zeros_like(acc)

    def bins(i, c):
        first = lax.rem(blk + NG - 2 * i, NG)
        second = lax.rem(blk + NG - 2 * i - 1, NG)

        @pl.when(i > 0)
        def _():
            copy_s(first, first).wait_recv()

        copy_s(second, second).wait_recv()
        acc[...] += bin_two(first, second)
        return c

    lax.fori_loop(0, NG // 2, bins, 0)
    dense[...] = acc[...].astype(BF16)
    for fetch in fetches[6:]:
        fetch.wait()

    def copy_a(e, slot):
        return pltpu.make_async_remote_copy(
            src_ref=cube.at[e],
            dst_ref=got_a.at[slot],
            send_sem=send_a.at[e],
            recv_sem=recv_a.at[slot],
            device_id=(blk, e),
            device_id_type=MESH,
        )

    cube[...] = (
        jnp.dot(psi2_v[...], dense[...], preferred_element_type=F32).astype(BF16).reshape(NB, 64, 256)
    )

    def start_a(i, c):
        e = lax.rem(beam + i, NB)
        copy_a(e, beam).start()
        return c

    lax.fori_loop(1, NB, start_a, 0)

    def settle_a(i, total):
        e = lax.rem(beam + NB - i, NB)
        copy_a(e, e).wait_recv()
        return total + got_a[e].astype(F32)

    x = lax.fori_loop(1, NB, settle_a, cube[beam].astype(F32)).astype(BF16)
    pq = jnp.dot(x, t1_v[...], preferred_element_type=F32)
    for a in range(4):
        p = pq[:, a * 256 : a * 256 + 128].reshape(8, 8, 128)
        q = pq[:, a * 256 + 128 : a * 256 + 256].reshape(8, 8, 128)
        ta, tb = tw_v[a, 0][None], tw_v[a, 1][None]
        mix[a * 128 : a * 128 + 64] = (p * ta + q * tb).reshape(64, 128).astype(BF16)
        mix[a * 128 + 64 : a * 128 + 128] = (p * tb - q * ta).reshape(64, 128).astype(BF16)
    spec[...] = jnp.dot(d2_v[...], mix[...], preferred_element_type=F32).reshape(NG, 8, 128)

    def copy_c(g, slot):
        return pltpu.make_async_remote_copy(
            src_ref=spec.at[g],
            dst_ref=got_c.at[slot],
            send_sem=send_c.at[g],
            recv_sem=recv_c.at[slot],
            device_id=(g, beam),
            device_id_type=MESH,
        )

    def start_c(i, c):
        copy_c(lax.rem(blk + i, NG), blk).start()
        return c

    lax.fori_loop(1, NG, start_c, 0)
    got_c[blk] = spec[blk]

    def settle_c(i, c):
        g = lax.rem(blk + NG - i, NG)
        copy_c(g, g).wait_recv()
        return c

    lax.fori_loop(1, NG, settle_c, 0)
    coef[...] = lax.dot_general(
        got_c[...].reshape(128, 128).astype(BF16), perm_v[...], (((0,), (0,)), ((), ())), preferred_element_type=F32
    ).astype(BF16)
    diagonal = (lax.broadcasted_iota(jnp.int32, (16, 1024), 0) >> 1) == (
        lax.broadcasted_iota(jnp.int32, (16, 1024), 1) >> 7
    )

    def copy_e(e, slot):
        return pltpu.make_async_remote_copy(
            src_ref=send_e.at[e],
            dst_ref=got_e.at[slot],
            send_sem=send_sem_e.at[e],
            recv_sem=recv_sem_e.at[slot],
            device_id=(blk, e),
            device_id_type=MESH,
        )

    def contract(i, c):
        e = lax.rem(beam + i, NB)
        load(e).wait()
        rows = coef[pl.ds(pl.multiple_of(e * 16, 16), 16), :].astype(F32)
        left = jnp.where(diagonal, jnp.concatenate([rows] * 8, axis=1), 0.0).astype(BF16)
        part = jnp.dot(left, wig[pl.ds(pl.multiple_of(e * 1024, 1024), 1024), :], preferred_element_type=F32)

        @pl.when(i < NB)
        def _():
            send_e[e] = part.astype(BF16)
            copy_e(e, beam).start()

        @pl.when(i == NB)
        def _():
            out[...] = part

        return c

    lax.fori_loop(1, NB + 1, contract, 0)

    def settle_e(i, c):
        e = lax.rem(beam + NB - i, NB)
        copy_e(e, e).wait_recv()
        out[...] += got_e[e].astype(F32)
        return c

    lax.fori_loop(1, NB, settle_e, 0)

    def sent_beam(i, c):
        e = lax.rem(beam + i, NB)
        copy_a(e, e).wait_send()
        copy_e(e, e).wait_send()
        return c

    def sent_blk(i, c):
        g = lax.rem(blk + i, NG)
        copy_s(g, g).wait_send()
        copy_c(g, g).wait_send()
        return c

    lax.fori_loop(1, NB, sent_beam, 0)
    lax.fori_loop(1, NG, sent_blk, 0)


ANY = pl.BlockSpec(memory_space=pl.ANY)


def shards(signal, weight, cycle, phi, psi, owner, wigner):
    block = lambda x: x.reshape(128, 128)
    dma = pltpu.SemaphoreType.DMA
    operands = (
        block(signal),
        block(weight),
        block(cycle),
        block(phi),
        block(psi),
        owner.reshape(1, 128),
        *tables(),
        wigner.reshape(64 * 128, L),
    )
    alm = pl.pallas_call(
        kernel,
        out_shape=pltpu.VMEM((16, L), F32),
        in_specs=[ANY] * len(operands),
        out_specs=pl.BlockSpec(memory_space=pltpu.VMEM),
        scratch_shapes=[
            *(pltpu.VMEM(x.shape, x.dtype) for x in operands),
            pltpu.VMEM((512, 128), BF16),
            pltpu.VMEM((NG, ROWS, 128), BF16),
            pltpu.VMEM((NG, ROWS, 128), BF16),
            pltpu.VMEM((512, 256), F32),
            pltpu.VMEM((512, 256), BF16),
            pltpu.VMEM((NB, 64, 256), BF16),
            pltpu.VMEM((NB, 64, 256), BF16),
            pltpu.VMEM((512, 128), BF16),
            pltpu.VMEM((NG, 8, 128), F32),
            pltpu.VMEM((NG, 8, 128), F32),
            pltpu.VMEM((128, 128), BF16),
            pltpu.VMEM((NB, 16, L), BF16),
            pltpu.VMEM((NB, 16, L), BF16),
            dma((11,)),
            dma((NB,)),
            dma((NG,)),
            dma((NG,)),
            dma((NB,)),
            dma((NB,)),
            dma((NG,)),
            dma((NG,)),
            dma((NB,)),
            dma((NB,)),
        ],
        compiler_params=pltpu.CompilerParams(
            collective_id=0, has_side_effects=True, vmem_limit_bytes=56 * 2**20
        ),
        name="sky_coefficients",
    )(*operands)
    return alm.reshape(8, 2, L)


def solution(mesh):
    return jax.shard_map(
        shards,
        mesh=mesh,
        in_specs=(
            P(("blk", "beam")),
            P(("blk", "beam")),
            P(("blk", "beam")),
            P(("blk", "beam")),
            P(("blk", "beam")),
            P(("blk", "beam"), None),
            P("blk", "beam", None, None),
        ),
        out_specs=P(("blk", "beam"), None, None),
        check_vma=False,
    )
```

```python
import math

import jax
import jax.numpy as jnp
import numpy as np
from jax import lax
from jax.experimental import pallas as pl
from jax.experimental.pallas import tpu as pltpu
from jax.sharding import PartitionSpec as P

MESH = pl.DeviceIdType.MESH
F32 = jnp.float32
BF16 = jnp.bfloat16
NG = 16
NB = 8
NPSI = 32
NPHI = 2048
CAP = 20
CHUNK = 4
NCH = CAP // CHUNK
ROWS = 16 * NCH
L = 1152


def tables():
    q = np.arange(NPSI)[:, None]
    j = np.arange(NPSI)[None, :]
    psi = np.where(
        q <= 16, np.cos(2 * math.pi * ((q * j) % 32) / 32), np.sin(2 * math.pi * (((q - 16) * j) % 32) / 32)
    ) / math.sqrt(32)
    psi2 = np.einsum("qj,tu,fg->qtfujg", psi, np.eye(2), np.eye(8)).reshape(512, 512)
    f1 = np.arange(64)[:, None]
    r = np.arange(64)[None, :]
    angle = 2 * math.pi * ((r * f1) % 64) / 64
    cs = np.stack([np.cos(angle), np.sin(angle)], axis=1)
    cs = np.repeat(cs[:, :, :, None], 2, axis=3).reshape(64, 256)
    t1 = np.einsum("ab,fn->afbn", np.eye(4), cs).reshape(256, 1024)
    f0 = np.arange(32)[:, None]
    turn = 2 * math.pi * (r * f0) / 2048
    tr, ti = np.cos(turn) / math.sqrt(NPHI), np.sin(turn) / math.sqrt(NPHI)
    a = np.stack([tr, ti], axis=2).reshape(4, 8, 128)
    b = np.stack([-ti, tr], axis=2).reshape(4, 8, 128)
    tw = np.stack([a, b], axis=1)
    blk = np.arange(NG)[:, None]
    outer = 2 * math.pi * ((blk * np.arange(32)[None, :]) % 32) / 32
    cos, sin = np.cos(outer).reshape(NG, 4, 8), np.sin(outer).reshape(NG, 4, 8)
    both = np.stack([cos, sin], axis=2)
    d2 = np.einsum("bayf,st->bsaytf", both, np.eye(8)).reshape(128, 512)
    row = np.arange(128)
    b_, q_, t_ = row // 8, row // 2 % 4, row % 2
    e = np.zeros((128, 128))
    e[row, q_ * 32 + 2 * b_ + t_] = 1
    return (
        jnp.asarray(psi2, BF16),
        jnp.asarray(t1, BF16),
        jnp.asarray(tw, F32),
        jnp.asarray(d2, BF16),
        jnp.asarray(e, BF16),
    )


def kernel(
    signal, weight, cycle, phi, psi, owner, psi2, t1, tw, d2, perm, wigner, out,
    signal_v, weight_v, cycle_v, phi_v, psi_v, owner_v, psi2_v, t1_v, tw_v, d2_v, perm_v, wig,
    data, sendbuf, got, acc, dense, cube, got_a, mix, spec, got_c, coef, send_e, got_e,
    in_sem, wig_sem, send_s, recv_s, send_a, recv_a, send_c, recv_c, send_sem_e, recv_sem_e,
):
    blk, beam = lax.axis_index("blk"), lax.axis_index("beam")
    barrier = pltpu.get_barrier_semaphore()

    sources = (signal, weight, cycle, phi, psi, owner, psi2, t1, tw, d2, perm)
    places = (signal_v, weight_v, cycle_v, phi_v, psi_v, owner_v, psi2_v, t1_v, tw_v, d2_v, perm_v)
    fetches = [pltpu.make_async_copy(a, b, in_sem.at[n]) for n, (a, b) in enumerate(zip(sources, places))]
    for fetch in fetches[5::-1]:
        fetch.start()

    def greet_blk(i, c):
        pl.semaphore_signal(barrier, inc=1, device_id=(lax.rem(blk + i, NG), beam), device_id_type=MESH)
        return c

    def greet_beam(i, c):
        pl.semaphore_signal(barrier, inc=1, device_id=(blk, lax.rem(beam + i, NB)), device_id_type=MESH)
        return c

    lax.fori_loop(1, NG, greet_blk, 0)
    lax.fori_loop(1, NB, greet_beam, 0)

    def load(e):
        rows = pl.ds(pl.multiple_of(e * 1024, 1024), 1024)
        return pltpu.make_async_copy(wigner.at[rows], wig.at[rows], wig_sem.at[e])

    def start_load(i, c):
        load(lax.rem(beam + i, NB)).start()
        return c

    fetches[5].wait()
    own = owner_v[...]
    hit = lax.broadcasted_iota(jnp.int32, (NG, 128), 0) == own
    upper = lax.broadcasted_iota(jnp.int32, (128, 128), 0) < lax.broadcasted_iota(jnp.int32, (128, 128), 1)
    before = jnp.dot(
        jnp.where(hit, 1.0, 0.0).astype(BF16), jnp.where(upper, 1.0, 0.0).astype(BF16), preferred_element_type=F32
    )
    within = jnp.sum(jnp.where(hit, before, 0.0), axis=0, keepdims=True).astype(jnp.int32)
    key = own * 1024 + within
    key = jnp.concatenate([key, key + 32, key + 64, key + 96], axis=1)
    at = lax.broadcasted_iota(jnp.int32, (ROWS, 512), 0)
    base = ((at >> 4) * CHUNK + (at & 3)) + ((at >> 2) & 3) * 32

    for fetch in fetches[:5]:
        fetch.wait()
    value = signal_v[...] * weight_v[...]
    zero = jnp.zeros_like(value)
    cyc = cycle_v[...]
    cell = phi_v[...]
    data[0:128] = jnp.where(cyc == 0, value, zero).astype(BF16)
    data[128:256] = jnp.where(cyc == 0, zero, value).astype(BF16)
    data[256:384] = (psi_v[...] * 8 + (cell & 7) + 1).astype(F32).astype(BF16)
    data[384:512] = (((cell >> 3) & 3) * 64 + (cell >> 5) + 1).astype(F32).astype(BF16)
    def copy_s(g, slot):
        return pltpu.make_async_remote_copy(
            src_ref=sendbuf.at[g],
            dst_ref=got.at[slot],
            send_sem=send_s.at[g],
            recv_sem=recv_s.at[slot],
            device_id=(g, beam),
            device_id_type=MESH,
        )

    def rows_of(i, c):
        chosen = jnp.concatenate([base + (4 * i + n) * 1024 for n in range(4)], axis=0) == key
        rows = jnp.dot(jnp.where(chosen, 1.0, 0.0).astype(BF16), data[...], preferred_element_type=F32)
        sendbuf[pl.ds(4 * i, 4)] = rows.astype(BF16).reshape(4, ROWS, 128)
        return c

    lax.fori_loop(0, NG // 4, rows_of, 0)
    pl.semaphore_wait(barrier, NG + NB - 2)

    def send(i, c):
        copy_s(lax.rem(blk + i, NG), blk).start()
        return c

    lax.fori_loop(1, NG, send, 0)
    got[blk] = sendbuf[blk]
    for fetch in fetches[6:]:
        fetch.start()
    lax.fori_loop(1, NB + 1, start_load, 0)

    cells = (lax.broadcasted_iota(jnp.int32, (256, 128), 0) + 1).astype(F32).astype(BF16)
    one, nil = jnp.ones((256, 128), BF16), jnp.zeros((256, 128), BF16)

    def bins_of(sources):
        low, high, right = [], [], []
        for source in sources:
            for n in range(NCH):
                tile = got[source, 16 * n : 16 * n + 16]
                for i in range(CHUNK):
                    same = tile[8 + i : 9 + i] == cells
                    low.append(jnp.where(same, jnp.broadcast_to(tile[i : i + 1], (256, 128)), nil))
                    high.append(jnp.where(same, jnp.broadcast_to(tile[4 + i : 5 + i], (256, 128)), nil))
                    right.append(jnp.where(tile[12 + i : 13 + i] == cells, one, nil))
        left = jnp.concatenate([jnp.concatenate(low, axis=1), jnp.concatenate(high, axis=1)], axis=0)
        return lax.dot_general(
            left, jnp.concatenate(right, axis=1), (((1,), (1,)), ((), ())), preferred_element_type=F32
        )

    acc[...] = jnp.zeros_like(acc)

    def bins(start, count):
        def step(i, c):
            sources = [lax.rem(blk + 2 * NG - start - count * i - n, NG) for n in range(count)]
            for n, g in enumerate(sources):
                if n == 0 and start == 0:

                    @pl.when(i > 0)
                    def _():
                        copy_s(g, g).wait_recv()
                else:
                    copy_s(g, g).wait_recv()
            acc[...] += bins_of(sources)
            return c

        return step

    lax.fori_loop(0, 4, bins(0, 1), 0)
    lax.fori_loop(0, 3, bins(4, 4), 0)
    dense[...] = acc[...].astype(BF16)
    for fetch in fetches[6:]:
        fetch.wait()

    def copy_a(e, slot):
        return pltpu.make_async_remote_copy(
            src_ref=cube.at[e],
            dst_ref=got_a.at[slot],
            send_sem=send_a.at[e],
            recv_sem=recv_a.at[slot],
            device_id=(blk, e),
            device_id_type=MESH,
        )

    cube[...] = (
        jnp.dot(psi2_v[...], dense[...], preferred_element_type=F32).astype(BF16).reshape(NB, 64, 256)
    )

    def far(i, sign):
        step = jnp.where(i < 3, 2, jnp.where(i < 5, 1, jnp.where(i < 7, 3, 0)))
        x, core = lax.div(beam, 2), lax.rem(beam, 2)
        return lax.rem(x + 4 + sign * step, 4) * 2 + lax.rem(core + i, 2)

    def start_a(i, c):
        e = far(i, 1)
        copy_a(e, beam).start()
        return c

    lax.fori_loop(1, NB, start_a, 0)

    def settle_a(i, total):
        e = far(i, -1)
        copy_a(e, e).wait_recv()
        return total + got_a[e].astype(F32)

    x = lax.fori_loop(1, NB, settle_a, cube[beam].astype(F32)).astype(BF16)
    pq = jnp.dot(x, t1_v[...], preferred_element_type=F32)
    for a in range(4):
        p = pq[:, a * 256 : a * 256 + 128].reshape(8, 8, 128)
        q = pq[:, a * 256 + 128 : a * 256 + 256].reshape(8, 8, 128)
        ta, tb = tw_v[a, 0][None], tw_v[a, 1][None]
        mix[a * 128 : a * 128 + 64] = (p * ta + q * tb).reshape(64, 128).astype(BF16)
        mix[a * 128 + 64 : a * 128 + 128] = (p * tb - q * ta).reshape(64, 128).astype(BF16)
    spec[...] = jnp.dot(d2_v[...], mix[...], preferred_element_type=F32).reshape(NG, 8, 128)

    def copy_c(g, slot):
        return pltpu.make_async_remote_copy(
            src_ref=spec.at[g],
            dst_ref=got_c.at[slot],
            send_sem=send_c.at[g],
            recv_sem=recv_c.at[slot],
            device_id=(g, beam),
            device_id_type=MESH,
        )

    def start_c(i, c):
        copy_c(lax.rem(blk + i, NG), blk).start()
        return c

    lax.fori_loop(1, NG, start_c, 0)
    got_c[blk] = spec[blk]

    def settle_c(i, c):
        g = lax.rem(blk + NG - i, NG)
        copy_c(g, g).wait_recv()
        return c

    lax.fori_loop(1, NG, settle_c, 0)
    coef[...] = lax.dot_general(
        got_c[...].reshape(128, 128).astype(BF16), perm_v[...], (((0,), (0,)), ((), ())), preferred_element_type=F32
    ).astype(BF16)
    diagonal = (lax.broadcasted_iota(jnp.int32, (16, 1024), 0) >> 1) == (
        lax.broadcasted_iota(jnp.int32, (16, 1024), 1) >> 7
    )

    def copy_e(e, slot):
        return pltpu.make_async_remote_copy(
            src_ref=send_e.at[e],
            dst_ref=got_e.at[slot],
            send_sem=send_sem_e.at[e],
            recv_sem=recv_sem_e.at[slot],
            device_id=(blk, e),
            device_id_type=MESH,
        )

    def contract(i, c):
        e = far(i, 1)
        load(e).wait()
        rows = coef[pl.ds(pl.multiple_of(e * 16, 16), 16), :].astype(F32)
        left = jnp.where(diagonal, jnp.concatenate([rows] * 8, axis=1), 0.0).astype(BF16)
        part = jnp.dot(left, wig[pl.ds(pl.multiple_of(e * 1024, 1024), 1024), :], preferred_element_type=F32)

        @pl.when(i < NB)
        def _():
            send_e[e] = part.astype(BF16)
            copy_e(e, beam).start()

        @pl.when(i == NB)
        def _():
            out[...] = part

        return c

    lax.fori_loop(1, NB + 1, contract, 0)

    def settle_e(i, c):
        e = far(i, -1)
        copy_e(e, e).wait_recv()
        out[...] += got_e[e].astype(F32)
        return c

    lax.fori_loop(1, NB, settle_e, 0)

    def sent_beam(i, c):
        e = lax.rem(beam + i, NB)
        copy_a(e, e).wait_send()
        copy_e(e, e).wait_send()
        return c

    def sent_blk(i, c):
        g = lax.rem(blk + i, NG)
        copy_s(g, g).wait_send()
        copy_c(g, g).wait_send()
        return c

    lax.fori_loop(1, NB, sent_beam, 0)
    lax.fori_loop(1, NG, sent_blk, 0)


ANY = pl.BlockSpec(memory_space=pl.ANY)


def shards(signal, weight, cycle, phi, psi, owner, wigner):
    block = lambda x: x.reshape(128, 128)
    dma = pltpu.SemaphoreType.DMA
    operands = (
        block(signal),
        block(weight),
        block(cycle),
        block(phi),
        block(psi),
        owner.reshape(1, 128),
        *tables(),
        wigner.reshape(64 * 128, L),
    )
    alm = pl.pallas_call(
        kernel,
        out_shape=pltpu.VMEM((16, L), F32),
        in_specs=[ANY] * len(operands),
        out_specs=pl.BlockSpec(memory_space=pltpu.VMEM),
        scratch_shapes=[
            *(pltpu.VMEM(x.shape, x.dtype) for x in operands),
            pltpu.VMEM((512, 128), BF16),
            pltpu.VMEM((NG, ROWS, 128), BF16),
            pltpu.VMEM((NG, ROWS, 128), BF16),
            pltpu.VMEM((512, 256), F32),
            pltpu.VMEM((512, 256), BF16),
            pltpu.VMEM((NB, 64, 256), BF16),
            pltpu.VMEM((NB, 64, 256), BF16),
            pltpu.VMEM((512, 128), BF16),
            pltpu.VMEM((NG, 8, 128), F32),
            pltpu.VMEM((NG, 8, 128), F32),
            pltpu.VMEM((128, 128), BF16),
            pltpu.VMEM((NB, 16, L), BF16),
            pltpu.VMEM((NB, 16, L), BF16),
            dma((11,)),
            dma((NB,)),
            dma((NG,)),
            dma((NG,)),
            dma((NB,)),
            dma((NB,)),
            dma((NG,)),
            dma((NG,)),
            dma((NB,)),
            dma((NB,)),
        ],
        compiler_params=pltpu.CompilerParams(
            collective_id=0, has_side_effects=True, vmem_limit_bytes=56 * 2**20
        ),
        name="sky_coefficients",
    )(*operands)
    return alm.reshape(8, 2, L)


def solution(mesh):
    return jax.shard_map(
        shards,
        mesh=mesh,
        in_specs=(
            P(("blk", "beam")),
            P(("blk", "beam")),
            P(("blk", "beam")),
            P(("blk", "beam")),
            P(("blk", "beam")),
            P(("blk", "beam"), None),
            P("blk", "beam", None, None),
        ),
        out_specs=P(("blk", "beam"), None, None),
        check_vma=False,
    )
```

```python
import math

import jax
import jax.numpy as jnp
import numpy as np
from jax import lax
from jax.experimental import pallas as pl
from jax.experimental.pallas import tpu as pltpu
from jax.sharding import PartitionSpec as P

MESH = pl.DeviceIdType.MESH
F32 = jnp.float32
BF16 = jnp.bfloat16
NG = 16
NB = 8
NPSI = 32
NPHI = 2048
CAP = 20
CHUNK = 4
NCH = CAP // CHUNK
ROWS = 16 * NCH
L = 1152


def tables():
    q = np.arange(NPSI)[:, None]
    j = np.arange(NPSI)[None, :]
    psi = np.where(
        q <= 16, np.cos(2 * math.pi * ((q * j) % 32) / 32), np.sin(2 * math.pi * (((q - 16) * j) % 32) / 32)
    ) / math.sqrt(32)
    psi2 = np.einsum("qj,fg->qfjg", psi, np.eye(8)).reshape(256, 256)
    f1 = np.arange(64)[:, None]
    r = np.arange(64)[None, :]
    angle = 2 * math.pi * ((r * f1) % 64) / 64
    cs = np.stack([np.cos(angle), np.sin(angle)], axis=1)
    cs = np.repeat(cs[:, :, :, None], 2, axis=3).reshape(64, 256)
    t1 = np.einsum("ab,fn->afbn", np.eye(4), cs).reshape(256, 1024)
    f0 = np.arange(32)[:, None]
    turn = 2 * math.pi * (r * f0) / 2048
    tr, ti = np.cos(turn) / math.sqrt(NPHI), np.sin(turn) / math.sqrt(NPHI)
    a = np.stack([tr, ti], axis=2).reshape(4, 8, 128)
    b = np.stack([-ti, tr], axis=2).reshape(4, 8, 128)
    tw = np.stack([a, b], axis=1)
    blk = np.arange(NG)[:, None]
    outer = 2 * math.pi * ((blk * np.arange(32)[None, :]) % 32) / 32
    cos, sin = np.cos(outer).reshape(NG, 4, 8), np.sin(outer).reshape(NG, 4, 8)
    both = np.stack([cos, sin], axis=2)
    d2 = np.einsum("bayf,st->bsaytf", both, np.eye(8)).reshape(128, 512)
    row = np.arange(128)
    b_, t_, q_ = row // 8, row // 4 % 2, row % 4
    e = np.zeros((128, 128))
    e[row, q_ * 32 + 2 * b_ + t_] = 1
    return (
        jnp.asarray(psi2, BF16),
        jnp.asarray(t1, BF16),
        jnp.asarray(tw, F32),
        jnp.asarray(d2, BF16),
        jnp.asarray(e, BF16),
    )


def kernel(
    signal, weight, cycle, phi, psi, owner, psi2, t1, tw, d2, perm, wigner, out,
    signal_v, weight_v, cycle_v, phi_v, psi_v, owner_v, psi2_v, t1_v, tw_v, d2_v, perm_v, wig,
    data, sendbuf, got, acc, cube, got_a, mix, spec, got_c, coef, send_e, got_e,
    in_sem, wig_sem, send_s, recv_s, send_a, recv_a, send_c, recv_c, send_sem_e, recv_sem_e,
):
    blk, beam = lax.axis_index("blk"), lax.axis_index("beam")
    barrier = pltpu.get_barrier_semaphore()

    sources = (signal, weight, cycle, phi, psi, owner, psi2, t1, tw, d2, perm)
    places = (signal_v, weight_v, cycle_v, phi_v, psi_v, owner_v, psi2_v, t1_v, tw_v, d2_v, perm_v)
    fetches = [pltpu.make_async_copy(a, b, in_sem.at[n]) for n, (a, b) in enumerate(zip(sources, places))]
    for fetch in fetches[5::-1]:
        fetch.start()

    def greet_blk(i, c):
        pl.semaphore_signal(barrier, inc=1, device_id=(lax.rem(blk + i, NG), beam), device_id_type=MESH)
        return c

    def greet_beam(i, c):
        pl.semaphore_signal(barrier, inc=1, device_id=(blk, lax.rem(beam + i, NB)), device_id_type=MESH)
        return c

    lax.fori_loop(1, NG, greet_blk, 0)
    lax.fori_loop(1, NB, greet_beam, 0)

    def load(e):
        rows = pl.ds(pl.multiple_of(e * 1024, 1024), 1024)
        return pltpu.make_async_copy(wigner.at[rows], wig.at[rows], wig_sem.at[e])

    def start_load(i, c):
        load(lax.rem(beam + i, NB)).start()
        return c

    fetches[5].wait()
    own = owner_v[...]
    hit = lax.broadcasted_iota(jnp.int32, (NG, 128), 0) == own
    upper = lax.broadcasted_iota(jnp.int32, (128, 128), 0) < lax.broadcasted_iota(jnp.int32, (128, 128), 1)
    before = jnp.dot(
        jnp.where(hit, 1.0, 0.0).astype(BF16), jnp.where(upper, 1.0, 0.0).astype(BF16), preferred_element_type=F32
    )
    within = jnp.sum(jnp.where(hit, before, 0.0), axis=0, keepdims=True).astype(jnp.int32)
    key = own * 1024 + within
    key = jnp.concatenate([key, key + 32, key + 64, key + 96], axis=1)
    at = lax.broadcasted_iota(jnp.int32, (ROWS, 512), 0)
    base = ((at >> 4) * CHUNK + (at & 3)) + ((at >> 2) & 3) * 32

    for fetch in fetches[:5]:
        fetch.wait()
    value = signal_v[...] * weight_v[...]
    zero = jnp.zeros_like(value)
    cyc = cycle_v[...]
    cell = phi_v[...]
    data[0:128] = jnp.where(cyc == 0, value, zero).astype(BF16)
    data[128:256] = jnp.where(cyc == 0, zero, value).astype(BF16)
    data[256:384] = (psi_v[...] * 8 + (cell & 7) + 1).astype(F32).astype(BF16)
    data[384:512] = (((cell >> 3) & 3) * 64 + (cell >> 5) + 1).astype(F32).astype(BF16)
    def copy_s(g, slot):
        return pltpu.make_async_remote_copy(
            src_ref=sendbuf.at[g],
            dst_ref=got.at[slot],
            send_sem=send_s.at[g],
            recv_sem=recv_s.at[slot],
            device_id=(g, beam),
            device_id_type=MESH,
        )

    def rows_of(i, c):
        chosen = jnp.concatenate([base + (4 * i + n) * 1024 for n in range(4)], axis=0) == key
        rows = jnp.dot(jnp.where(chosen, 1.0, 0.0).astype(BF16), data[...], preferred_element_type=F32)
        sendbuf[pl.ds(4 * i, 4)] = rows.astype(BF16).reshape(4, ROWS, 128)
        return c

    lax.fori_loop(0, NG // 4, rows_of, 0)
    pl.semaphore_wait(barrier, NG + NB - 2)

    def send(i, c):
        copy_s(lax.rem(blk + i, NG), blk).start()
        return c

    lax.fori_loop(1, NG, send, 0)
    got[blk] = sendbuf[blk]
    for fetch in fetches[6:]:
        fetch.start()
    lax.fori_loop(1, NB + 1, start_load, 0)

    cells = (lax.broadcasted_iota(jnp.int32, (256, 128), 0) + 1).astype(F32).astype(BF16)
    one, nil = jnp.ones((256, 128), BF16), jnp.zeros((256, 128), BF16)

    def bins_of(sources):
        low, high, right = [], [], []
        for source in sources:
            for n in range(NCH):
                tile = got[source, 16 * n : 16 * n + 16]
                for i in range(CHUNK):
                    same = tile[8 + i : 9 + i] == cells
                    low.append(jnp.where(same, jnp.broadcast_to(tile[i : i + 1], (256, 128)), nil))
                    high.append(jnp.where(same, jnp.broadcast_to(tile[4 + i : 5 + i], (256, 128)), nil))
                    right.append(jnp.where(tile[12 + i : 13 + i] == cells, one, nil))
        left = jnp.concatenate([jnp.concatenate(low, axis=1), jnp.concatenate(high, axis=1)], axis=0)
        return lax.dot_general(
            left, jnp.concatenate(right, axis=1), (((1,), (1,)), ((), ())), preferred_element_type=F32
        )

    acc[...] = jnp.zeros_like(acc)

    def bins(start, count):
        def step(i, c):
            sources = [lax.rem(blk + 2 * NG - start - count * i - n, NG) for n in range(count)]
            for n, g in enumerate(sources):
                if n == 0 and start == 0:

                    @pl.when(i > 0)
                    def _():
                        copy_s(g, g).wait_recv()
                else:
                    copy_s(g, g).wait_recv()
            acc[...] += bins_of(sources)
            return c

        return step

    lax.fori_loop(0, 4, bins(0, 1), 0)
    lax.fori_loop(0, 2, bins(4, 6), 0)
    for fetch in fetches[6:]:
        fetch.wait()
    for t in range(2):
        half = jnp.dot(psi2_v[...], acc[256 * t : 256 * t + 256].astype(BF16), preferred_element_type=F32)
        cube[:, 32 * t : 32 * t + 32, :] = half.astype(BF16).reshape(NB, 32, 256)

    def copy_a(e, slot):
        return pltpu.make_async_remote_copy(
            src_ref=cube.at[e],
            dst_ref=got_a.at[slot],
            send_sem=send_a.at[e],
            recv_sem=recv_a.at[slot],
            device_id=(blk, e),
            device_id_type=MESH,
        )

    def far(i, sign):
        step = jnp.where(i < 3, 2, jnp.where(i < 5, 1, jnp.where(i < 7, 3, 0)))
        x, core = lax.div(beam, 2), lax.rem(beam, 2)
        return lax.rem(x + 4 + sign * step, 4) * 2 + lax.rem(core + i, 2)

    def start_a(i, c):
        e = far(i, 1)
        copy_a(e, beam).start()
        return c

    lax.fori_loop(1, NB, start_a, 0)

    def settle_a(i, total):
        e = far(i, -1)
        copy_a(e, e).wait_recv()
        return total + got_a[e].astype(F32)

    x = lax.fori_loop(1, NB, settle_a, cube[beam].astype(F32)).astype(BF16)
    pq = jnp.dot(x, t1_v[...], preferred_element_type=F32)
    for a in range(4):
        p = pq[:, a * 256 : a * 256 + 128].reshape(8, 8, 128)
        q = pq[:, a * 256 + 128 : a * 256 + 256].reshape(8, 8, 128)
        ta, tb = tw_v[a, 0][None], tw_v[a, 1][None]
        mix[a * 128 : a * 128 + 64] = (p * ta + q * tb).reshape(64, 128).astype(BF16)
        mix[a * 128 + 64 : a * 128 + 128] = (p * tb - q * ta).reshape(64, 128).astype(BF16)
    spec[...] = jnp.dot(d2_v[...], mix[...], preferred_element_type=F32).reshape(NG, 8, 128)

    def copy_c(g, slot):
        return pltpu.make_async_remote_copy(
            src_ref=spec.at[g],
            dst_ref=got_c.at[slot],
            send_sem=send_c.at[g],
            recv_sem=recv_c.at[slot],
            device_id=(g, beam),
            device_id_type=MESH,
        )

    def start_c(i, c):
        copy_c(lax.rem(blk + i, NG), blk).start()
        return c

    lax.fori_loop(1, NG, start_c, 0)
    got_c[blk] = spec[blk]

    def settle_c(i, c):
        g = lax.rem(blk + NG - i, NG)
        copy_c(g, g).wait_recv()
        return c

    lax.fori_loop(1, NG, settle_c, 0)
    coef[...] = lax.dot_general(
        got_c[...].reshape(128, 128).astype(BF16), perm_v[...], (((0,), (0,)), ((), ())), preferred_element_type=F32
    ).astype(BF16)
    diagonal = (lax.broadcasted_iota(jnp.int32, (16, 1024), 0) >> 1) == (
        lax.broadcasted_iota(jnp.int32, (16, 1024), 1) >> 7
    )

    def copy_e(e, slot):
        return pltpu.make_async_remote_copy(
            src_ref=send_e.at[e],
            dst_ref=got_e.at[slot],
            send_sem=send_sem_e.at[e],
            recv_sem=recv_sem_e.at[slot],
            device_id=(blk, e),
            device_id_type=MESH,
        )

    def contract(i, c):
        e = far(i, 1)
        load(e).wait()
        rows = coef[pl.ds(pl.multiple_of(e * 16, 16), 16), :].astype(F32)
        left = jnp.where(diagonal, jnp.concatenate([rows] * 8, axis=1), 0.0).astype(BF16)
        part = jnp.dot(left, wig[pl.ds(pl.multiple_of(e * 1024, 1024), 1024), :], preferred_element_type=F32)

        @pl.when(i < NB)
        def _():
            send_e[e] = part.astype(BF16)
            copy_e(e, beam).start()

        @pl.when(i == NB)
        def _():
            out[...] = part

        return c

    lax.fori_loop(1, NB + 1, contract, 0)

    def settle_e(i, c):
        e = far(i, -1)
        copy_e(e, e).wait_recv()
        out[...] += got_e[e].astype(F32)
        return c

    lax.fori_loop(1, NB, settle_e, 0)

    def sent_beam(i, c):
        e = lax.rem(beam + i, NB)
        copy_a(e, e).wait_send()
        copy_e(e, e).wait_send()
        return c

    def sent_blk(i, c):
        g = lax.rem(blk + i, NG)
        copy_s(g, g).wait_send()
        copy_c(g, g).wait_send()
        return c

    lax.fori_loop(1, NB, sent_beam, 0)
    lax.fori_loop(1, NG, sent_blk, 0)


ANY = pl.BlockSpec(memory_space=pl.ANY)


def shards(signal, weight, cycle, phi, psi, owner, wigner):
    block = lambda x: x.reshape(128, 128)
    dma = pltpu.SemaphoreType.DMA
    operands = (
        block(signal),
        block(weight),
        block(cycle),
        block(phi),
        block(psi),
        owner.reshape(1, 128),
        *tables(),
        wigner.reshape(64 * 128, L),
    )
    alm = pl.pallas_call(
        kernel,
        out_shape=pltpu.VMEM((16, L), F32),
        in_specs=[ANY] * len(operands),
        out_specs=pl.BlockSpec(memory_space=pltpu.VMEM),
        scratch_shapes=[
            *(pltpu.VMEM(x.shape, x.dtype) for x in operands),
            pltpu.VMEM((512, 128), BF16),
            pltpu.VMEM((NG, ROWS, 128), BF16),
            pltpu.VMEM((NG, ROWS, 128), BF16),
            pltpu.VMEM((512, 256), F32),
            pltpu.VMEM((NB, 64, 256), BF16),
            pltpu.VMEM((NB, 64, 256), BF16),
            pltpu.VMEM((512, 128), BF16),
            pltpu.VMEM((NG, 8, 128), F32),
            pltpu.VMEM((NG, 8, 128), F32),
            pltpu.VMEM((128, 128), BF16),
            pltpu.VMEM((NB, 16, L), BF16),
            pltpu.VMEM((NB, 16, L), BF16),
            dma((11,)),
            dma((NB,)),
            dma((NG,)),
            dma((NG,)),
            dma((NB,)),
            dma((NB,)),
            dma((NG,)),
            dma((NG,)),
            dma((NB,)),
            dma((NB,)),
        ],
        compiler_params=pltpu.CompilerParams(
            collective_id=0, has_side_effects=True, vmem_limit_bytes=56 * 2**20
        ),
        name="sky_coefficients",
    )(*operands)
    return alm.reshape(8, 2, L)


def solution(mesh):
    return jax.shard_map(
        shards,
        mesh=mesh,
        in_specs=(
            P(("blk", "beam")),
            P(("blk", "beam")),
            P(("blk", "beam")),
            P(("blk", "beam")),
            P(("blk", "beam")),
            P(("blk", "beam"), None),
            P("blk", "beam", None, None),
        ),
        out_specs=P(("blk", "beam"), None, None),
        check_vma=False,
    )
```

```python
import math

import jax
import jax.numpy as jnp
import numpy as np
from jax import lax
from jax.experimental import pallas as pl
from jax.experimental.pallas import tpu as pltpu
from jax.sharding import PartitionSpec as P

MESH = pl.DeviceIdType.MESH
F32 = jnp.float32
BF16 = jnp.bfloat16
NG = 16
NB = 8
NPSI = 32
NPHI = 2048
CAP = 20
CHUNK = 4
NCH = CAP // CHUNK
ROWS = 16 * NCH
L = 1152


def tables():
    q = np.arange(NPSI)[:, None]
    j = np.arange(NPSI)[None, :]
    psi = np.where(
        q <= 16, np.cos(2 * math.pi * ((q * j) % 32) / 32), np.sin(2 * math.pi * (((q - 16) * j) % 32) / 32)
    ) / math.sqrt(32)
    psi2 = np.einsum("qj,fg->qfjg", psi, np.eye(8)).reshape(256, 256)
    f1 = np.arange(64)[:, None]
    r = np.arange(64)[None, :]
    angle = 2 * math.pi * ((r * f1) % 64) / 64
    cs = np.stack([np.cos(angle), np.sin(angle)], axis=1)
    cs = np.repeat(cs[:, :, :, None], 2, axis=3).reshape(64, 256)
    t1 = np.einsum("ab,fn->afbn", np.eye(4), cs).reshape(256, 1024)
    f0 = np.arange(32)[:, None]
    turn = 2 * math.pi * (r * f0) / 2048
    tr, ti = np.cos(turn) / math.sqrt(NPHI), np.sin(turn) / math.sqrt(NPHI)
    a = np.stack([tr, ti], axis=2).reshape(4, 8, 128)
    b = np.stack([-ti, tr], axis=2).reshape(4, 8, 128)
    tw = np.stack([a, b], axis=1)
    blk = np.arange(NG)[:, None]
    outer = 2 * math.pi * ((blk * np.arange(32)[None, :]) % 32) / 32
    cos, sin = np.cos(outer).reshape(NG, 4, 8), np.sin(outer).reshape(NG, 4, 8)
    both = np.stack([cos, sin], axis=2)
    d2 = np.einsum("bayf,st->bsaytf", both, np.eye(8)).reshape(128, 512)
    row = np.arange(128)
    b_, t_, q_ = row // 8, row // 4 % 2, row % 4
    e = np.zeros((128, 128))
    e[row, q_ * 32 + 2 * b_ + t_] = 1
    return (
        jnp.asarray(psi2, BF16),
        jnp.asarray(t1, BF16),
        jnp.asarray(tw, F32),
        jnp.asarray(d2, BF16),
        jnp.asarray(e, BF16),
    )


def kernel(
    signal, weight, cycle, phi, psi, owner, psi2, t1, tw, d2, perm, wigner, out,
    signal_v, weight_v, cycle_v, phi_v, psi_v, owner_v, psi2_v, t1_v, tw_v, d2_v, perm_v, wig,
    data, sendbuf, got, acc, cube, got_a, mix, spec, got_c, coef, send_e, got_e,
    in_sem, wig_sem, send_s, recv_s, send_a, recv_a, send_c, recv_c, send_sem_e, recv_sem_e,
):
    blk, beam = lax.axis_index("blk"), lax.axis_index("beam")
    barrier = pltpu.get_barrier_semaphore()

    sources = (signal, weight, cycle, phi, psi, owner, psi2, t1, tw, d2, perm)
    places = (signal_v, weight_v, cycle_v, phi_v, psi_v, owner_v, psi2_v, t1_v, tw_v, d2_v, perm_v)
    fetches = [pltpu.make_async_copy(a, b, in_sem.at[n]) for n, (a, b) in enumerate(zip(sources, places))]
    for fetch in fetches[5::-1]:
        fetch.start()

    def greet_blk(i, c):
        pl.semaphore_signal(barrier, inc=1, device_id=(lax.rem(blk + i, NG), beam), device_id_type=MESH)
        return c

    def greet_beam(i, c):
        pl.semaphore_signal(barrier, inc=1, device_id=(blk, lax.rem(beam + i, NB)), device_id_type=MESH)
        return c

    lax.fori_loop(1, NG, greet_blk, 0)
    lax.fori_loop(1, NB, greet_beam, 0)

    def load(e):
        rows = pl.ds(pl.multiple_of(e * 1024, 1024), 1024)
        return pltpu.make_async_copy(wigner.at[rows], wig.at[rows], wig_sem.at[e])

    def start_load(i, c):
        load(lax.rem(beam + i, NB)).start()
        return c

    fetches[5].wait()
    own = owner_v[...]
    hit = lax.broadcasted_iota(jnp.int32, (NG, 128), 0) == own
    upper = lax.broadcasted_iota(jnp.int32, (128, 128), 0) < lax.broadcasted_iota(jnp.int32, (128, 128), 1)
    before = jnp.dot(
        jnp.where(hit, 1.0, 0.0).astype(BF16), jnp.where(upper, 1.0, 0.0).astype(BF16), preferred_element_type=F32
    )
    within = jnp.sum(jnp.where(hit, before, 0.0), axis=0, keepdims=True).astype(jnp.int32)
    key = own * 1024 + within
    key = jnp.concatenate([key, key + 32, key + 64, key + 96], axis=1)
    at = lax.broadcasted_iota(jnp.int32, (ROWS, 512), 0)
    base = ((at >> 4) * CHUNK + (at & 3)) + ((at >> 2) & 3) * 32

    for fetch in fetches[:5]:
        fetch.wait()
    value = signal_v[...] * weight_v[...]
    zero = jnp.zeros_like(value)
    cyc = cycle_v[...]
    cell = phi_v[...]
    data[0:128] = jnp.where(cyc == 0, value, zero).astype(BF16)
    data[128:256] = jnp.where(cyc == 0, zero, value).astype(BF16)
    data[256:384] = (psi_v[...] * 8 + (cell & 7) + 1).astype(F32).astype(BF16)
    data[384:512] = (((cell >> 3) & 3) * 64 + (cell >> 5) + 1).astype(F32).astype(BF16)
    def copy_s(g, slot):
        return pltpu.make_async_remote_copy(
            src_ref=sendbuf.at[g],
            dst_ref=got.at[slot],
            send_sem=send_s.at[g],
            recv_sem=recv_s.at[slot],
            device_id=(g, beam),
            device_id_type=MESH,
        )

    def rows_of(i, c):
        chosen = jnp.concatenate([base + (4 * i + n) * 1024 for n in range(4)], axis=0) == key
        rows = jnp.dot(jnp.where(chosen, 1.0, 0.0).astype(BF16), data[...], preferred_element_type=F32)
        sendbuf[pl.ds(4 * i, 4)] = rows.astype(BF16).reshape(4, ROWS, 128)
        return c

    lax.fori_loop(0, NG // 4, rows_of, 0)
    pl.semaphore_wait(barrier, NG + NB - 2)

    def send(i, c):
        copy_s(lax.rem(blk + i, NG), blk).start()
        return c

    lax.fori_loop(1, NG, send, 0)
    got[blk] = sendbuf[blk]
    for fetch in fetches[6:]:
        fetch.start()
    lax.fori_loop(1, NB + 1, start_load, 0)

    cells = (lax.broadcasted_iota(jnp.int32, (256, 128), 0) + 1).astype(F32).astype(BF16)
    one, nil = jnp.ones((256, 128), BF16), jnp.zeros((256, 128), BF16)

    def bins_of(sources):
        low, high, right = [], [], []
        for source in sources:
            for n in range(NCH):
                tile = got[source, 16 * n : 16 * n + 16]
                for i in range(CHUNK):
                    same = tile[8 + i : 9 + i] == cells
                    low.append(jnp.where(same, jnp.broadcast_to(tile[i : i + 1], (256, 128)), nil))
                    high.append(jnp.where(same, jnp.broadcast_to(tile[4 + i : 5 + i], (256, 128)), nil))
                    right.append(jnp.where(tile[12 + i : 13 + i] == cells, one, nil))
        left = jnp.concatenate([jnp.concatenate(low, axis=1), jnp.concatenate(high, axis=1)], axis=0)
        return lax.dot_general(
            left, jnp.concatenate(right, axis=1), (((1,), (1,)), ((), ())), preferred_element_type=F32
        )

    acc[...] = jnp.zeros_like(acc)

    def bins(start, count):
        def step(i, c):
            sources = [lax.rem(blk + 2 * NG - start - count * i - n, NG) for n in range(count)]
            for n, g in enumerate(sources):
                if n == 0 and start == 0:

                    @pl.when(i > 0)
                    def _():
                        copy_s(g, g).wait_recv()
                else:
                    copy_s(g, g).wait_recv()
            acc[...] += bins_of(sources)
            return c

        return step

    lax.fori_loop(0, 4, bins(0, 1), 0)
    lax.fori_loop(0, 2, bins(4, 6), 0)
    for fetch in fetches[6:]:
        fetch.wait()
    for t in range(2):
        half = jnp.dot(psi2_v[...], acc[256 * t : 256 * t + 256].astype(BF16), preferred_element_type=F32)
        cube[:, 32 * t : 32 * t + 32, :] = half.astype(BF16).reshape(NB, 32, 256)

    def copy_a(e, slot):
        return pltpu.make_async_remote_copy(
            src_ref=cube.at[e],
            dst_ref=got_a.at[slot],
            send_sem=send_a.at[e],
            recv_sem=recv_a.at[slot],
            device_id=(blk, e),
            device_id_type=MESH,
        )

    def far(i, sign):
        step = jnp.where(i < 3, 2, jnp.where(i < 5, 1, jnp.where(i < 7, 3, 0)))
        x, core = lax.div(beam, 2), lax.rem(beam, 2)
        return lax.rem(x + 4 + sign * step, 4) * 2 + lax.rem(core + i, 2)

    def start_a(i, c):
        e = far(i, 1)
        copy_a(e, beam).start()
        return c

    lax.fori_loop(1, NB, start_a, 0)

    def settle_a(i, total):
        e = far(i, -1)
        copy_a(e, e).wait_recv()
        return total + got_a[e].astype(F32)

    x = lax.fori_loop(1, NB, settle_a, cube[beam].astype(F32)).astype(BF16)
    pq = jnp.dot(x, t1_v[...], preferred_element_type=F32)
    for a in range(4):
        p = pq[:, a * 256 : a * 256 + 128].reshape(8, 8, 128)
        q = pq[:, a * 256 + 128 : a * 256 + 256].reshape(8, 8, 128)
        ta, tb = tw_v[a, 0][None], tw_v[a, 1][None]
        mix[a * 128 : a * 128 + 64] = (p * ta + q * tb).reshape(64, 128).astype(BF16)
        mix[a * 128 + 64 : a * 128 + 128] = (p * tb - q * ta).reshape(64, 128).astype(BF16)
    spec[...] = jnp.dot(d2_v[...], mix[...], preferred_element_type=F32).reshape(NG, 8, 128)

    def copy_c(g, slot):
        return pltpu.make_async_remote_copy(
            src_ref=spec.at[g],
            dst_ref=got_c.at[slot],
            send_sem=send_c.at[g],
            recv_sem=recv_c.at[slot],
            device_id=(g, beam),
            device_id_type=MESH,
        )

    def start_c(i, c):
        copy_c(lax.rem(blk + i, NG), blk).start()
        return c

    lax.fori_loop(1, NG, start_c, 0)
    got_c[blk] = spec[blk]

    def settle_c(i, c):
        g = lax.rem(blk + NG - i, NG)
        copy_c(g, g).wait_recv()
        return c

    lax.fori_loop(1, NG, settle_c, 0)
    rows = lax.dot_general(
        got_c[...].reshape(128, 128).astype(BF16), perm_v[...], (((0,), (0,)), ((), ())), preferred_element_type=F32
    )
    diagonal = ((lax.broadcasted_iota(jnp.int32, (128, 1024), 0) >> 1) & 7) == (
        lax.broadcasted_iota(jnp.int32, (128, 1024), 1) >> 7
    )
    coef[...] = jnp.where(diagonal, jnp.concatenate([rows] * 8, axis=1), 0.0).astype(BF16)

    def copy_e(e, slot):
        return pltpu.make_async_remote_copy(
            src_ref=send_e.at[e],
            dst_ref=got_e.at[slot],
            send_sem=send_sem_e.at[e],
            recv_sem=recv_sem_e.at[slot],
            device_id=(blk, e),
            device_id_type=MESH,
        )

    def contract(i, c):
        e = far(i, 1)
        load(e).wait()
        left = coef[pl.ds(pl.multiple_of(e * 16, 16), 16), :]
        part = jnp.dot(left, wig[pl.ds(pl.multiple_of(e * 1024, 1024), 1024), :], preferred_element_type=F32)

        @pl.when(i < NB)
        def _():
            send_e[e] = part.astype(BF16)
            copy_e(e, beam).start()

        @pl.when(i == NB)
        def _():
            out[...] = part

        return c

    lax.fori_loop(1, NB + 1, contract, 0)

    def sent_beam(i, c):
        e = lax.rem(beam + i, NB)
        copy_a(e, e).wait_send()
        copy_e(e, e).wait_send()
        return c

    def sent_blk(i, c):
        g = lax.rem(blk + i, NG)
        copy_s(g, g).wait_send()
        copy_c(g, g).wait_send()
        return c

    lax.fori_loop(1, NB, sent_beam, 0)
    lax.fori_loop(1, NG, sent_blk, 0)

    def settle_e(i, c):
        e = far(i, -1)
        copy_e(e, e).wait_recv()
        out[...] += got_e[e].astype(F32)
        return c

    lax.fori_loop(1, NB, settle_e, 0)


ANY = pl.BlockSpec(memory_space=pl.ANY)


def shards(signal, weight, cycle, phi, psi, owner, wigner):
    block = lambda x: x.reshape(128, 128)
    dma = pltpu.SemaphoreType.DMA
    operands = (
        block(signal),
        block(weight),
        block(cycle),
        block(phi),
        block(psi),
        owner.reshape(1, 128),
        *tables(),
        wigner.reshape(64 * 128, L),
    )
    alm = pl.pallas_call(
        kernel,
        out_shape=pltpu.VMEM((16, L), F32),
        in_specs=[ANY] * len(operands),
        out_specs=pl.BlockSpec(memory_space=pltpu.VMEM),
        scratch_shapes=[
            *(pltpu.VMEM(x.shape, x.dtype) for x in operands),
            pltpu.VMEM((512, 128), BF16),
            pltpu.VMEM((NG, ROWS, 128), BF16),
            pltpu.VMEM((NG, ROWS, 128), BF16),
            pltpu.VMEM((512, 256), F32),
            pltpu.VMEM((NB, 64, 256), BF16),
            pltpu.VMEM((NB, 64, 256), BF16),
            pltpu.VMEM((512, 128), BF16),
            pltpu.VMEM((NG, 8, 128), F32),
            pltpu.VMEM((NG, 8, 128), F32),
            pltpu.VMEM((128, 1024), BF16),
            pltpu.VMEM((NB, 16, L), BF16),
            pltpu.VMEM((NB, 16, L), BF16),
            dma((11,)),
            dma((NB,)),
            dma((NG,)),
            dma((NG,)),
            dma((NB,)),
            dma((NB,)),
            dma((NG,)),
            dma((NG,)),
            dma((NB,)),
            dma((NB,)),
        ],
        compiler_params=pltpu.CompilerParams(
            collective_id=0, has_side_effects=True, vmem_limit_bytes=56 * 2**20
        ),
        name="sky_coefficients",
    )(*operands)
    return alm.reshape(8, 2, L)


def solution(mesh):
    return jax.shard_map(
        shards,
        mesh=mesh,
        in_specs=(
            P(("blk", "beam")),
            P(("blk", "beam")),
            P(("blk", "beam")),
            P(("blk", "beam")),
            P(("blk", "beam")),
            P(("blk", "beam"), None),
            P("blk", "beam", None, None),
        ),
        out_specs=P(("blk", "beam"), None, None),
        check_vma=False,
    )
```
